32 devices in a mesh: sample: 4 (over x, core), freq: 8 (over z, y).
Axes of the slice: x: 2, y: 2, z: 4, core: 2. Of those that a mesh axis runs over, the one named last changes fastest.
Arguments:
- images: bfloat16 [256, 32, 32, 128], P(('sample', 'freq')), may hold values from -6 to 6
- cotangent: bfloat16 [256, 32, 32, 128], P(('sample', 'freq')), may hold values from -6 to 6
- kernel: float32 [3, 3, 128, 128], replicated, may hold values from -0.022097087 to 0.022097087
Outputs:
- outputs: bfloat16 [256, 32, 32, 128], P(('sample', 'freq'))
- kernel_grad: float32 [3, 3, 128, 128], replicated
The draws below stay inside these ranges and needn't reach their ends.
All inputs are finite; a program needn't handle non-finite values.
Results may differ from the reference program's by a relative error of at most 0.0064.
Values may be sent and summed in bfloat16 or wider, within the bound.
No kernel may reach another device: no remote copies, remote signals or barrier semaphores. Data moves between devices by JAX's collectives and lax.ppermute only.
A program may use at most 128 MiB of HBM per device.

```python
import math
import jax
import jax.numpy as jnp
from jax import lax

C = 128
SIDE = 32
TAPS = 3
NS_STEPS = 2
IMG_DEV = 8
HALF = 17
IMAGES = 256


def draw_kernel(key, part):
    bound_value = 0.1 * 3.0 ** 0.5 / C ** 0.5
    return jax.random.uniform(key, (TAPS, TAPS, C, C), jnp.float32, -bound_value, bound_value)


def block_levels(stream_key, dims, cuts, low, high):
    loudness, own = 1.0, jax.random.fold_in(stream_key, 6)
    for dim, blocks in cuts:
        draws = jnp.exp(jax.random.uniform(jax.random.fold_in(own, dim), (blocks,), jnp.float32, low / len(cuts), high / len(cuts)))
        loudness = loudness * jnp.repeat(draws, dims[dim] // blocks).reshape([-1 if axis == dim else 1 for axis in range(len(dims))])
    return loudness


def centred(own_key, shape, scale, limit, cuts=(), kind=jnp.bfloat16):
    values = scale * jax.random.normal(own_key, shape, jnp.float32)
    if cuts:
        values = values * block_levels(own_key, shape, cuts, -0.22, 0.18)
    return jnp.clip(values, -limit, limit).astype(kind)


def setup_inputs(seed: int = 0) -> dict:
    splits = jax.random.split(jax.random.key(seed), 4)
    return {
        "images": centred(splits[0], (IMAGES, SIDE, SIDE, C), 1.0, 6.0, ((0, 32),)),
        "cotangent": centred(splits[1], (IMAGES, SIDE, SIDE, C), 1.0, 6.0, ((0, 32),)),
        "kernel": draw_kernel(jax.random.fold_in(splits[3], 71), 0),
    }


HIGHEST = lax.Precision.HIGHEST


def angle_tables(side_cells, half_cells):
    position = jnp.arange(side_cells, dtype=jnp.int32)
    columns = jnp.arange(half_cells, dtype=jnp.int32)
    across = (position[:, None] * columns[None, :]) % side_cells
    square = (position[:, None] * position[None, :]) % side_cells
    radians = 2.0 * math.pi / side_cells
    return radians * across.astype(jnp.float32), radians * square.astype(jnp.float32)


def forward_spectrum(pictures, across_angle, square_angle):
    number = pictures.shape[0]
    side_cells = pictures.shape[1]
    channels = pictures.shape[3]
    half_cells = across_angle.shape[1]
    row_table = jnp.concatenate([jnp.cos(across_angle), -jnp.sin(across_angle)], axis=1)
    partial_sum = jnp.einsum("nhwc,wk->nhkc", pictures.astype(jnp.float32), row_table, precision=HIGHEST)
    partial_sum = partial_sum.reshape(number, side_cells, 2, half_cells, channels)
    cosine = jnp.cos(square_angle)
    sine_table = jnp.sin(square_angle)
    rotation = jnp.stack([jnp.stack([cosine, sine_table]), jnp.stack([-sine_table, cosine])])
    spectrum = jnp.einsum("abuh,nhbvc->nuvac", rotation, partial_sum, precision=HIGHEST)
    return spectrum.reshape(number, side_cells, half_cells, 2 * channels).astype(jnp.bfloat16)


def inverse_spectrum(spectrum, across_angle, square_angle):
    number = spectrum.shape[0]
    side_cells = spectrum.shape[1]
    half_cells = spectrum.shape[2]
    channels = spectrum.shape[3] // 2
    pieces = spectrum.astype(jnp.float32).reshape(number, side_cells, half_cells, 2, channels)
    cosine = jnp.cos(square_angle)
    sine_table = jnp.sin(square_angle)
    rotation = jnp.stack([jnp.stack([cosine, -sine_table]), jnp.stack([sine_table, cosine])])
    column_sum = jnp.einsum("abuh,nuvbc->nhavc", rotation, pieces, precision=HIGHEST)
    frequency = jnp.arange(half_cells, dtype=jnp.int32)
    boundary = (frequency == 0) | (frequency == side_cells // 2)
    weights = jnp.where(boundary, 1.0, 2.0).astype(jnp.float32) / (side_cells * side_cells)
    back_table = jnp.concatenate([jnp.cos(across_angle).T * weights[:, None], -jnp.sin(across_angle).T * weights[:, None]], axis=0)
    result = jnp.einsum("nhkc,kw->nhwc", column_sum.reshape(number, side_cells, 2 * half_cells, channels), back_table, precision=HIGHEST)
    return result.astype(jnp.bfloat16)


def tap_angles(row_numbers, side_cells, half_cells, tap_count):
    offsets = jnp.arange(tap_count, dtype=jnp.int32) - (tap_count - 1) // 2
    columns = jnp.arange(half_cells, dtype=jnp.int32)
    phases = (row_numbers[:, None, None, None] * offsets[None, None, :, None] + columns[None, :, None, None] * offsets[None, None, None, :]) % side_cells
    phases = phases.reshape(row_numbers.shape[0] * half_cells, tap_count * tap_count)
    return (2.0 * math.pi / side_cells) * phases.astype(jnp.float32)


def skew_matrix(kernel, angles):
    flattened = kernel.reshape(kernel.shape[0] * kernel.shape[1], kernel.shape[2], kernel.shape[3])
    real_part = jnp.einsum("ft,toi->foi", jnp.cos(angles), flattened, precision=HIGHEST)
    imag_part = -jnp.einsum("ft,toi->foi", jnp.sin(angles), flattened, precision=HIGHEST)
    return (real_part - jnp.swapaxes(real_part, 1, 2), imag_part + jnp.swapaxes(imag_part, 1, 2))


def rounded(matrix):
    return lax.optimization_barrier(matrix.astype(jnp.bfloat16)).astype(jnp.float32)


def low_multiply(former, latter):
    return jnp.einsum("fij,fjk->fik", rounded(former), rounded(latter))


def full_multiply(former, latter):
    return jnp.einsum("fij,fjk->fik", former, latter, precision=HIGHEST)


def complex_product(former, latter, multiply):
    real_out = multiply(former[0], latter[0]) - multiply(former[1], latter[1])
    imag_out = multiply(former[0], latter[1]) + multiply(former[1], latter[0])
    return (real_out, imag_out)


def adjoint(matrix):
    return (jnp.swapaxes(matrix[0], 1, 2), -jnp.swapaxes(matrix[1], 1, 2))


def cayley_deviation(skew_part):
    deviation = (-skew_part[0], -skew_part[1])
    for iteration in range(NS_STEPS):
        cross_term = complex_product(skew_part, deviation, low_multiply)
        residue = (-(skew_part[0] + deviation[0] + cross_term[0]), -(skew_part[1] + deviation[1] + cross_term[1]))
        update = complex_product(deviation, residue, low_multiply)
        deviation = (deviation[0] + residue[0] + update[0], deviation[1] + residue[1] + update[1])
    return deviation


def embedded(deviation):
    doubled_real = (2.0 * deviation[0]).astype(jnp.bfloat16)
    doubled_imag = (2.0 * deviation[1]).astype(jnp.bfloat16)
    upper_half = jnp.concatenate([doubled_real, -doubled_imag], axis=2)
    lower_half = jnp.concatenate([doubled_imag, doubled_real], axis=2)
    return jnp.concatenate([upper_half, lower_half], axis=1)


def grad_factor(side_cells, half_cells, total_images):
    frequency = jnp.arange(half_cells, dtype=jnp.int32)
    boundary = (frequency == 0) | (frequency == side_cells // 2)
    return jnp.where(boundary, 2.0, 4.0).astype(jnp.float32) / (side_cells * side_cells * total_images)


def skew_gradient(spec_grad, deviation):
    conjugate = adjoint(deviation)
    partial_term = complex_product(spec_grad, conjugate, full_multiply)
    partial_term = (spec_grad[0] + partial_term[0], spec_grad[1] + partial_term[1])
    outer_term = complex_product(conjugate, partial_term, full_multiply)
    return (-(partial_term[0] + outer_term[0]), -(partial_term[1] + outer_term[1]))


def kernel_piece(skew_grad, angles, tap_count):
    sym_real = skew_grad[0] - jnp.swapaxes(skew_grad[0], 1, 2)
    sym_imag = skew_grad[1] + jnp.swapaxes(skew_grad[1], 1, 2)
    piece_sum = jnp.einsum("ft,foi->toi", jnp.cos(angles), sym_real, precision=HIGHEST) - jnp.einsum("ft,foi->toi", jnp.sin(angles), sym_imag, precision=HIGHEST)
    return piece_sum.reshape(tap_count, tap_count, sym_real.shape[1], sym_real.shape[2])


def reference(images, cotangent, kernel):
    across_angle, square_angle = angle_tables(SIDE, HALF)
    block_count = IMAGES // IMG_DEV

    def forward_block(pictures):
        return forward_spectrum(pictures, across_angle, square_angle)

    image_spectrum = lax.map(forward_block, images.reshape(block_count, IMG_DEV, SIDE, SIDE, C)).reshape(IMAGES, SIDE, HALF, 2 * C)
    tangent_spectrum = lax.map(forward_block, cotangent.reshape(block_count, IMG_DEV, SIDE, SIDE, C)).reshape(IMAGES, SIDE, HALF, 2 * C)
    factor = grad_factor(SIDE, HALF, IMAGES)

    def row_work(row_index):
        image_row = lax.dynamic_index_in_dim(image_spectrum, row_index, 1, keepdims=False)
        tangent_row = lax.dynamic_index_in_dim(tangent_spectrum, row_index, 1, keepdims=False)
        angles = tap_angles(jnp.reshape(row_index, (1,)).astype(jnp.int32), SIDE, HALF, TAPS)
        skew_part = skew_matrix(kernel, angles)
        deviation = cayley_deviation(skew_part)
        operator = embedded(deviation)
        image_float = image_row.astype(jnp.float32)
        answer_row = (image_float + jnp.einsum("nfj,fkj->nfk", image_float, operator.astype(jnp.float32))).astype(jnp.bfloat16)
        outer_sum = jnp.einsum("nfk,nfj->fkj", tangent_row.astype(jnp.float32), image_float)
        grad_real = (outer_sum[:, :C, :C] + outer_sum[:, C:, C:]) * factor[:, None, None]
        grad_imag = (outer_sum[:, C:, :C] - outer_sum[:, :C, C:]) * factor[:, None, None]
        skew_grad = skew_gradient((grad_real, grad_imag), deviation)
        return answer_row, kernel_piece(skew_grad, angles, TAPS)

    answer_rows, kernel_parts = lax.map(row_work, jnp.arange(SIDE, dtype=jnp.int32))
    answer_spectrum = jnp.transpose(answer_rows, (1, 0, 2, 3))

    def inverse_block(spectrum):
        return inverse_spectrum(spectrum, across_angle, square_angle)

    outputs = lax.map(inverse_block, answer_spectrum.reshape(block_count, IMG_DEV, SIDE, HALF, 2 * C)).reshape(IMAGES, SIDE, SIDE, C)
    kernel_grad = jnp.sum(kernel_parts, axis=0)
    return outputs, kernel_grad
```

```python
import functools
import math

import jax
import jax.numpy as jnp
import numpy as np
from jax import lax
from jax.experimental import pallas as pl
from jax.experimental.pallas import tpu as pltpu
from jax.sharding import PartitionSpec as P

AXES = ("sample", "freq")
APPLICATIONS = 7
CHAINS = 2
VMEM_LIMIT = 56 * 1024 * 1024


def split_table(table):
    high = table.astype(jnp.bfloat16)
    low = (table - high.astype(np.float64)).astype(jnp.bfloat16)
    return high, low


def forward_table(number, side):
    place = np.arange(side)
    table = np.zeros((side, side))
    table[0] = 1.0
    table[1] = np.cos(np.pi * place)
    for slot in range(1, side // 2):
        angle = 2.0 * math.pi * ((slot * place) % side) / side
        table[2 * slot] = np.cos(angle)
        table[2 * slot + 1] = -np.sin(angle)
    full = np.einsum("kw,nm->knmw", table, np.eye(number))
    return full.reshape(side * number, number * side)


def inverse_table(number, side):
    place = np.arange(side)
    table = np.zeros((side, side))
    table[:, 0] = 2.0 / side
    table[:, 1] = 2.0 / side * np.cos(np.pi * place)
    for slot in range(1, side // 2):
        angle = 2.0 * math.pi * ((slot * place) % side) / side
        table[:, 2 * slot] = 4.0 / side * np.cos(angle)
        table[:, 2 * slot + 1] = -4.0 / side * np.sin(angle)
    full = np.einsum("wk,nm->nwkm", table, np.eye(number))
    return full.reshape(number * side, side * number)


def slot_factors(side):
    rows = [[1.0, -1.0, 0.0, 1.0 / side]]
    for slot in range(1, side // 2):
        angle = 2.0 * math.pi * slot / side
        rows.append([math.cos(angle), math.cos(angle), math.sin(angle), 2.0 / side])
    table = np.array(rows)
    weighted = table[:, :3] * table[:, 3:]
    return np.concatenate([table, weighted], axis=1).astype(np.float32)


def dot(left, right):
    return jnp.dot(left, right, preferred_element_type=jnp.float32)


def main_kernel(
    scale,
    factor_ref,
    x_ref,
    t_ref,
    kernel_ref,
    high_ref,
    low_ref,
    dev_ref,
    grad_ref,
    base_ref,
    held_ref,
    weight_ref,
    taps_ref,
    sums_ref,
):
    number, side, _, channels = x_ref.shape
    slots = side // 2
    wide = 2 * channels

    for a in range(3):
        flipped = [kernel_ref[a, b].T - kernel_ref[2 - a, 2 - b] for b in range(3)]
        taps_ref[a, 0] = -flipped[1]
        taps_ref[a, 1] = -(flipped[2] + flipped[0])
        taps_ref[a, 2] = flipped[2] - flipped[0]
    sums_ref[...] = jnp.zeros_like(sums_ref)

    def transform(h, carry):
        rows = jnp.concatenate(
            [
                x_ref[:, h].reshape(number * side, channels),
                t_ref[:, h].reshape(number * side, channels),
            ],
            axis=1,
        )
        result = dot(high_ref[...], rows) + dot(low_ref[...], rows)
        result = result.reshape(slots, 2, number, wide)
        base_ref[:, h, :number, :channels] = result[:, 0, :, :channels]
        base_ref[:, h, :number, channels:] = result[:, 1, :, :channels]
        base_ref[:, h, number:, :channels] = result[:, 0, :, channels:]
        base_ref[:, h, number:, channels:] = result[:, 1, :, channels:]
        return carry

    lax.fori_loop(0, side, transform, 0, unroll=2)

    def store_held(chain, parity, start, rows):
        held = rows.astype(jnp.bfloat16)
        count = rows.shape[0]
        held_ref[chain, parity, start + 1 : start + 1 + count] = held
        if start == 0:
            held_ref[chain, parity, side + 1] = held[0]
        if start + count == side:
            held_ref[chain, parity, 0] = held[count - 1]

    def prepare(chain, slot):
        cos_top, cos_low, sine = (factor_ref[slot, j] for j in range(3))
        for a in range(3):
            first, second = taps_ref[a, 0], taps_ref[a, 1]
            cross = sine * taps_ref[a, 2]
            row = a * wide
            weight_ref[chain, row : row + channels, :channels] = (
                first + cos_top * second
            ).astype(jnp.bfloat16)
            weight_ref[chain, row + channels : row + wide, channels:] = (
                first + cos_low * second
            ).astype(jnp.bfloat16)
            weight_ref[chain, row : row + channels, channels:] = cross.astype(jnp.bfloat16)
            weight_ref[chain, row + channels : row + wide, :channels] = (-cross).astype(
                jnp.bfloat16
            )
        store_held(chain, 0, 0, base_ref[slot])

    def apply(chain, slot, step):
        parity = step % 2
        left = jnp.concatenate(
            [
                held_ref[chain, parity, 2 - a : 2 - a + side].reshape(side * 2 * number, wide)
                for a in range(3)
            ],
            axis=1,
        )
        moved = dot(left, weight_ref[chain]).reshape(side, 2 * number, wide)
        base = base_ref[slot]
        x_new = base[:, :number] + moved[:, :number]
        if step % 2 == 0:
            t_new = moved[:, number:] - base[:, number:]
        else:
            t_new = moved[:, number:] + base[:, number:]
        return moved, x_new, t_new

    def finish(chain, slot, moved, x_new, t_new):
        dev_ref[:, 2 * slot] = moved[:, :number, :channels]
        dev_ref[:, 2 * slot + 1] = moved[:, :number, channels:]
        left = t_new.reshape(side * number, wide).astype(jnp.bfloat16)
        around = jnp.concatenate([x_new[side - 1 :], x_new, x_new[:1]], axis=0)
        weight, top, low, sine = (factor_ref[slot, j] for j in range(3, 7))
        for a in range(3):
            right = around[2 - a : 2 - a + side].reshape(side * number, wide).astype(jnp.bfloat16)
            outer = lax.dot_general(
                left, right, (((0,), (0,)), ((), ())), preferred_element_type=jnp.float32
            )
            upper, lower = outer[:channels, :channels], outer[channels:, channels:]
            sums_ref[a, 0] += weight * (upper + lower)
            sums_ref[a, 1] += top * upper + low * lower
            sums_ref[a, 2] += sine * (outer[channels:, :channels] - outer[:channels, channels:])

    def work(pair, carry):
        chosen = [pair * CHAINS + chain for chain in range(CHAINS)]
        for chain in range(CHAINS):
            prepare(chain, chosen[chain])
        for step in range(APPLICATIONS):
            for chain in range(CHAINS):
                moved, x_new, t_new = apply(chain, chosen[chain], step)
                if step < APPLICATIONS - 1:
                    store_held(
                        chain, (step + 1) % 2, 0, jnp.concatenate([x_new, t_new], axis=1)
                    )
                else:
                    finish(chain, chosen[chain], moved, x_new, t_new)
        return carry

    lax.fori_loop(0, slots // CHAINS, work, 0)

    def correlation(a, b):
        if b == 1:
            return sums_ref[a, 0]
        if b == 2:
            return sums_ref[a, 1] - sums_ref[a, 2]
        return sums_ref[a, 1] + sums_ref[a, 2]

    for place, (a, b) in enumerate(((1, 1), (1, 2), (2, 0), (2, 1), (2, 2))):
        grad_ref[place] = scale * (correlation(a, b) - correlation(2 - a, 2 - b).T)


def inverse_kernel(x_ref, dev_ref, high_ref, low_ref, out_ref):
    number, side, _, channels = x_ref.shape

    def transform(pair, carry):
        rows = jnp.concatenate(
            [dev_ref[2 * pair + j].reshape(side * number, channels) for j in range(2)], axis=1
        )
        high = rows.astype(jnp.bfloat16)
        low = (rows - high.astype(jnp.float32)).astype(jnp.bfloat16)
        result = dot(high_ref[...], high) + dot(low_ref[...], high) + dot(high_ref[...], low)
        for j in range(2):
            h = 2 * pair + j
            piece = result[:, j * channels : (j + 1) * channels]
            piece = piece.reshape(number, side, channels) + x_ref[:, h].astype(jnp.float32)
            out_ref[:, h] = piece.astype(jnp.bfloat16)
        return carry

    lax.fori_loop(0, side // 2, transform, 0, unroll=2)


def mirror_kernel(sum_ref, grad_ref):
    for place, (a, b) in enumerate(((1, 1), (1, 2), (2, 0), (2, 1), (2, 2))):
        piece = sum_ref[place]
        grad_ref[a, b] = piece
        if place:
            grad_ref[2 - a, 2 - b] = -piece.T


def whole(memory_space=pltpu.VMEM):
    return pl.BlockSpec(memory_space=memory_space)


def device_sum(partial):
    count = lax.axis_size("sample") * lax.axis_size("freq")
    rows = partial.reshape(-1, partial.shape[-1])
    share = -(-rows.shape[0] // count)
    padded = jnp.pad(rows, ((0, share * count - rows.shape[0]), (0, 0)))
    terms = lax.all_to_all(
        padded.reshape(count, share, -1), AXES, split_axis=0, concat_axis=0, tiled=True
    )
    own = jnp.sum(terms, axis=0, keepdims=True)
    shares = lax.all_to_all(
        jnp.broadcast_to(own, terms.shape), AXES, split_axis=0, concat_axis=0, tiled=True
    )
    return shares.reshape(padded.shape)[: rows.shape[0]].reshape(partial.shape)


def per_device(images, cotangent, kernel):
    number, side, _, channels = images.shape
    slots = side // 2
    wide = 2 * channels
    total = number * lax.axis_size("sample") * lax.axis_size("freq")
    forward_high, forward_low = split_table(forward_table(number, side))
    inverse_high, inverse_low = split_table(inverse_table(number, side))
    rows = side * 2 * number
    params = pltpu.CompilerParams(vmem_limit_bytes=VMEM_LIMIT)
    deviation, partial = pl.pallas_call(
        functools.partial(main_kernel, 2.0 / total),
        out_shape=(
            jax.ShapeDtypeStruct((side, side, number, channels), jnp.float32),
            jax.ShapeDtypeStruct((5, channels, channels), jnp.float32),
        ),
        in_specs=[whole(pltpu.SMEM)] + [whole()] * 5,
        out_specs=(whole(), whole()),
        scratch_shapes=[
            pltpu.VMEM((slots, side, 2 * number, wide), jnp.float32),
            pltpu.VMEM((CHAINS, 2, side + 2, 2 * number, wide), jnp.bfloat16),
            pltpu.VMEM((CHAINS, 3 * wide, wide), jnp.bfloat16),
            pltpu.VMEM((3, 3, channels, channels), jnp.float32),
            pltpu.VMEM((3, 3, channels, channels), jnp.float32),
        ],
        compiler_params=params,
        cost_estimate=pl.CostEstimate(
            flops=2 * APPLICATIONS * slots * rows * 3 * wide * wide,
            bytes_accessed=12 * 1024 * 1024,
            transcendentals=0,
        ),
        name="horner_and_gradient",
    )(jnp.asarray(slot_factors(side)), images, cotangent, kernel, jnp.asarray(forward_high), jnp.asarray(forward_low))
    summed = device_sum(partial)
    outputs = pl.pallas_call(
        inverse_kernel,
        out_shape=jax.ShapeDtypeStruct(images.shape, jnp.bfloat16),
        in_specs=[whole()] * 4,
        out_specs=whole(),
        compiler_params=params,
        cost_estimate=pl.CostEstimate(
            flops=6 * side * side * number * side * number * channels,
            bytes_accessed=8 * 1024 * 1024,
            transcendentals=0,
        ),
        name="inverse_transform",
    )(images, deviation, jnp.asarray(inverse_high), jnp.asarray(inverse_low))
    kernel_grad = pl.pallas_call(
        mirror_kernel,
        out_shape=jax.ShapeDtypeStruct(kernel.shape, jnp.float32),
        in_specs=[whole()],
        out_specs=whole(),
        name="mirror_taps",
    )(summed)
    return (outputs, kernel_grad)


def solution(mesh):
    split = P(AXES, None, None, None)
    return jax.shard_map(
        per_device,
        mesh=mesh,
        in_specs=(split, split, P()),
        out_specs=(split, P()),
        check_vma=False,
    )
```

```python
import functools
import math

import jax
import jax.numpy as jnp
import numpy as np
from jax import lax
from jax.experimental import pallas as pl
from jax.experimental.pallas import tpu as pltpu
from jax.sharding import PartitionSpec as P

AXES = ("sample", "freq")
APPLICATIONS = 7
CHAINS = 2
IN_PARTS = 4
UNROLL = 4
GROUPS = 2
HALF_TAPS = ((1, 1), (1, 2), (2, 0), (2, 1), (2, 2))
VMEM_LIMIT = 56 * 1024 * 1024


def split_table(table):
    high = table.astype(jnp.bfloat16)
    low = (table - high.astype(np.float64)).astype(jnp.bfloat16)
    return high, low


def forward_table(number, side):
    place = np.arange(side)
    table = np.zeros((side, side))
    table[0] = 1.0
    table[1] = np.cos(np.pi * place)
    for slot in range(1, side // 2):
        angle = 2.0 * math.pi * ((slot * place) % side) / side
        table[2 * slot] = np.cos(angle)
        table[2 * slot + 1] = -np.sin(angle)
    full = np.einsum("kw,nm->knmw", table, np.eye(number))
    return full.reshape(side * number, number * side)


def inverse_table(number, side):
    place = np.arange(side)
    table = np.zeros((side, side))
    table[:, 0] = 2.0 / side
    table[:, 1] = 2.0 / side * np.cos(np.pi * place)
    for slot in range(1, side // 2):
        angle = 2.0 * math.pi * ((slot * place) % side) / side
        table[:, 2 * slot] = 4.0 / side * np.cos(angle)
        table[:, 2 * slot + 1] = -4.0 / side * np.sin(angle)
    full = np.einsum("wk,nm->nwkm", table, np.eye(number))
    return full.reshape(number * side, side * number)


def slot_factors(side):
    rows = [[1.0, -1.0, 0.0, 1.0 / side]]
    for slot in range(1, side // 2):
        angle = 2.0 * math.pi * slot / side
        rows.append([math.cos(angle), math.cos(angle), math.sin(angle), 2.0 / side])
    table = np.array(rows)
    weighted = table[:, :3] * table[:, 3:]
    return np.concatenate([table, weighted], axis=1).astype(np.float32)


def dot(left, right):
    return jnp.dot(left, right, preferred_element_type=jnp.float32)


def main_kernel(
    scale,
    factor_ref,
    x_hbm,
    t_hbm,
    kernel_ref,
    high_ref,
    low_ref,
    dev_hbm,
    grad_ref,
    x_ref,
    t_ref,
    base_ref,
    held_ref,
    weight_ref,
    taps_ref,
    sums_ref,
    dev_ref,
    left_ref,
    right_ref,
    in_sems,
    out_sems,
):
    number, side, _, channels = x_ref.shape
    slots = side // 2
    wide = 2 * channels
    part = side // IN_PARTS

    def incoming(index, place):
        source, target = ((x_hbm, x_ref), (t_hbm, t_ref))[index]
        rows = pl.ds(place * part, part)
        return pltpu.make_async_copy(
            source.at[:, rows], target.at[:, rows], in_sems.at[index, place]
        )

    def outgoing(slot):
        return pltpu.make_async_copy(dev_ref.at[slot], dev_hbm.at[slot], out_sems.at[slot])

    for place in range(IN_PARTS):
        for index in range(2):
            incoming(index, place).start()

    for a in range(3):
        flipped = [kernel_ref[a, b].T - kernel_ref[2 - a, 2 - b] for b in range(3)]
        taps_ref[a, 0] = -flipped[1]
        taps_ref[a, 1] = -(flipped[2] + flipped[0])
        taps_ref[a, 2] = flipped[2] - flipped[0]
    sums_ref[...] = jnp.zeros_like(sums_ref)
    left_ref[...] = jnp.zeros_like(left_ref)
    right_ref[...] = jnp.zeros_like(right_ref)

    def transform(h, carry):
        rows = jnp.concatenate(
            [
                x_ref[:, h].reshape(number * side, channels),
                t_ref[:, h].reshape(number * side, channels),
            ],
            axis=1,
        )
        result = dot(high_ref[...], rows) + dot(low_ref[...], rows)
        result = result.reshape(slots, 2, number, wide)
        base_ref[:, h, :number, :channels] = result[:, 0, :, :channels]
        base_ref[:, h, :number, channels:] = result[:, 1, :, :channels]
        base_ref[:, h, number:, :channels] = result[:, 0, :, channels:]
        base_ref[:, h, number:, channels:] = result[:, 1, :, channels:]
        return carry

    def store_held(chain, parity, rows):
        held = rows.astype(jnp.bfloat16)
        held_ref[chain, parity, 1 : 1 + side] = held
        held_ref[chain, parity, side + 1] = held[0]
        held_ref[chain, parity, 0] = held[side - 1]

    def prepare_taps(buffer, slot, a):
        cos_top, cos_low, sine = (factor_ref[slot, j] for j in range(3))
        first, second = taps_ref[a, 0], taps_ref[a, 1]
        cross = (sine * taps_ref[a, 2]).astype(jnp.bfloat16)
        row = a * wide
        middle, last = row + channels, row + wide
        weight_ref[buffer, row:middle, :channels] = (first + cos_top * second).astype(jnp.bfloat16)
        weight_ref[buffer, middle:last, channels:] = (first + cos_low * second).astype(jnp.bfloat16)
        weight_ref[buffer, row:middle, channels:] = cross
        weight_ref[buffer, middle:last, :channels] = -cross

    def apply(buffer, chain, parity, slot, step):
        left = jnp.concatenate(
            [
                held_ref[chain, parity, 2 - a : 2 - a + side].reshape(side * 2 * number, wide)
                for a in range(3)
            ],
            axis=1,
        )
        moved = dot(left, weight_ref[buffer]).reshape(side, 2 * number, wide)
        base = base_ref[slot]
        x_new = base[:, :number] + moved[:, :number]
        if step % 2 == 0:
            t_new = moved[:, number:] - base[:, number:]
        else:
            t_new = moved[:, number:] + base[:, number:]
        return moved, x_new, t_new

    def finish(buffer, slot, moved, x_new, t_new):
        dev_ref[slot, :, 0] = moved[:, :number, :channels]
        dev_ref[slot, :, 1] = moved[:, :number, channels:]
        left_ref[buffer] = t_new.reshape(side * number, wide).astype(jnp.bfloat16)
        around = jnp.concatenate([x_new[side - 1 :], x_new, x_new[:1]], axis=0)
        for a in range(3):
            right = around[2 - a : 2 - a + side].reshape(side * number, wide)
            right_ref[buffer, :, a * wide : (a + 1) * wide] = right.astype(jnp.bfloat16)

    def products(buffer, slot):
        weight, top, low, sine = (factor_ref[slot, j] for j in range(3, 7))
        outer_all = lax.dot_general(
            left_ref[buffer],
            right_ref[buffer],
            (((0,), (0,)), ((), ())),
            preferred_element_type=jnp.float32,
        )
        for a in range(3):
            outer = outer_all[:, a * wide : (a + 1) * wide]
            upper, lower = outer[:channels, :channels], outer[channels:, channels:]
            sums_ref[a, 0] += weight * (upper + lower)
            sums_ref[a, 1] += top * upper + low * lower
            sums_ref[a, 2] += sine * (outer[channels:, :channels] - outer[:channels, channels:])

    def work(group, odd):
        here, first = (CHAINS, 1) if odd else (0, 0)
        there = CHAINS - here
        before = jnp.maximum((group - 1) * CHAINS, 0)
        after = jnp.minimum((group + 1) * CHAINS, slots - CHAINS)
        jobs = [
            functools.partial(products, there + chain, before + chain) for chain in range(CHAINS)
        ] + [
            functools.partial(prepare_taps, there + chain, after + chain, a)
            for chain in range(CHAINS)
            for a in range(3)
        ]
        share = -(-len(jobs) // ((APPLICATIONS - 1) * CHAINS))
        for step in range(APPLICATIONS):
            for chain in range(CHAINS):
                slot = group * CHAINS + chain
                result = apply(here + chain, chain, (first + step) % 2, slot, step)
                if step < APPLICATIONS - 1:
                    store_held(
                        chain, (first + step + 1) % 2, jnp.concatenate(result[1:], axis=1)
                    )
                else:
                    finish(here + chain, slot, *result)
                if step == APPLICATIONS - 2:
                    store_held(chain, 1 - first, base_ref[after + chain])
                for job in jobs[:share]:
                    job()
                jobs = jobs[share:]

    for place in range(IN_PARTS):
        for index in range(2):
            incoming(index, place).wait()
        lax.fori_loop(place * part, (place + 1) * part, transform, 0, unroll=UNROLL)
    for chain in range(CHAINS):
        for a in range(3):
            prepare_taps(chain, chain, a)
        store_held(chain, 0, base_ref[chain])

    def some_groups(index, carry):
        for member in range(GROUPS):
            work(GROUPS * index + member, member % 2 == 1)
        for slot in range(GROUPS * CHAINS):
            outgoing(index * GROUPS * CHAINS + slot).start()
        return carry

    lax.fori_loop(0, slots // (GROUPS * CHAINS), some_groups, 0)
    for chain in range(CHAINS):
        products(CHAINS + chain, slots - CHAINS + chain)

    def correlation(a, b):
        if b == 1:
            return sums_ref[a, 0]
        if b == 2:
            return sums_ref[a, 1] - sums_ref[a, 2]
        return sums_ref[a, 1] + sums_ref[a, 2]

    for place, (a, b) in enumerate(HALF_TAPS):
        piece = scale * (correlation(a, b) - correlation(2 - a, 2 - b).T)
        grad_ref[place * channels : (place + 1) * channels] = piece.astype(grad_ref.dtype)
    rows = len(HALF_TAPS) * channels
    if grad_ref.shape[0] > rows:
        grad_ref[rows:] = jnp.zeros((grad_ref.shape[0] - rows, channels), grad_ref.dtype)
    for slot in range(slots):
        outgoing(slot).wait()


def inverse_kernel(x_ref, dev_ref, high_ref, low_ref, out_ref):
    number, side, _, channels = x_ref.shape

    def transform(pair, carry):
        rows = jnp.concatenate(
            [dev_ref[:, 2 * pair + j].reshape(side * number, channels) for j in range(2)], axis=1
        )
        high = rows.astype(jnp.bfloat16)
        low = (rows - high.astype(jnp.float32)).astype(jnp.bfloat16)
        result = dot(high_ref[...], high) + dot(low_ref[...], high) + dot(high_ref[...], low)
        for j in range(2):
            h = 2 * pair + j
            piece = result[:, j * channels : (j + 1) * channels]
            piece = piece.reshape(number, side, channels) + x_ref[:, h].astype(jnp.float32)
            out_ref[:, h] = piece.astype(jnp.bfloat16)
        return carry

    lax.fori_loop(0, side // 2, transform, 0, unroll=2)


def mirror_kernel(sum_ref, grad_ref):
    channels = sum_ref.shape[1]
    for place, (a, b) in enumerate(HALF_TAPS):
        piece = sum_ref[place * channels : (place + 1) * channels].astype(jnp.float32)
        grad_ref[a, b] = piece
        if place:
            grad_ref[2 - a, 2 - b] = -piece.T


def whole(memory_space=pltpu.VMEM):
    return pl.BlockSpec(memory_space=memory_space)


def device_sum(partial, count):
    terms = lax.all_to_all(
        partial.reshape(count, -1, partial.shape[1]), AXES, split_axis=0, concat_axis=0, tiled=True
    )
    own = jnp.sum(terms.astype(jnp.float32), axis=0, keepdims=True).astype(partial.dtype)
    shares = lax.all_to_all(
        jnp.broadcast_to(own, terms.shape), AXES, split_axis=0, concat_axis=0, tiled=True
    )
    return shares.reshape(partial.shape)


def per_device(images, cotangent, kernel):
    number, side, _, channels = images.shape
    slots = side // 2
    wide = 2 * channels
    count = lax.axis_size("sample") * lax.axis_size("freq")
    share = -(-len(HALF_TAPS) * channels // (8 * count)) * 8
    forward_high, forward_low = split_table(forward_table(number, side))
    inverse_high, inverse_low = split_table(inverse_table(number, side))
    rows = side * 2 * number
    params = pltpu.CompilerParams(vmem_limit_bytes=VMEM_LIMIT)
    deviation, partial = pl.pallas_call(
        functools.partial(main_kernel, 2.0 / (number * count)),
        out_shape=(
            jax.ShapeDtypeStruct((slots, side, 2, number, channels), jnp.float32),
            jax.ShapeDtypeStruct((count * share, channels), jnp.bfloat16),
        ),
        in_specs=[whole(pltpu.SMEM), whole(pl.ANY), whole(pl.ANY)] + [whole()] * 3,
        out_specs=(whole(pl.ANY), whole()),
        scratch_shapes=[
            pltpu.VMEM(images.shape, jnp.bfloat16),
            pltpu.VMEM(images.shape, jnp.bfloat16),
            pltpu.VMEM((slots, side, 2 * number, wide), jnp.float32),
            pltpu.VMEM((CHAINS, 2, side + 2, 2 * number, wide), jnp.bfloat16),
            pltpu.VMEM((2 * CHAINS, 3 * wide, wide), jnp.bfloat16),
            pltpu.VMEM((3, 3, channels, channels), jnp.float32),
            pltpu.VMEM((3, 3, channels, channels), jnp.float32),
            pltpu.VMEM((slots, side, 2, number, channels), jnp.float32),
            pltpu.VMEM((2 * CHAINS, side * number, wide), jnp.bfloat16),
            pltpu.VMEM((2 * CHAINS, side * number, 3 * wide), jnp.bfloat16),
            pltpu.SemaphoreType.DMA((2, IN_PARTS)),
            pltpu.SemaphoreType.DMA((slots,)),
        ],
        compiler_params=params,
        cost_estimate=pl.CostEstimate(
            flops=2 * APPLICATIONS * slots * rows * 3 * wide * wide,
            bytes_accessed=12 * 1024 * 1024,
            transcendentals=0,
        ),
        name="horner_and_gradient",
    )(
        jnp.asarray(slot_factors(side)),
        images,
        cotangent,
        kernel,
        jnp.asarray(forward_high),
        jnp.asarray(forward_low),
    )
    summed = device_sum(partial, count)
    outputs = pl.pallas_call(
        inverse_kernel,
        out_shape=jax.ShapeDtypeStruct(images.shape, jnp.bfloat16),
        in_specs=[whole()] * 4,
        out_specs=whole(),
        compiler_params=params,
        cost_estimate=pl.CostEstimate(
            flops=6 * side * side * number * side * number * channels,
            bytes_accessed=8 * 1024 * 1024,
            transcendentals=0,
        ),
        name="inverse_transform",
    )(images, deviation, jnp.asarray(inverse_high), jnp.asarray(inverse_low))
    kernel_grad = pl.pallas_call(
        mirror_kernel,
        out_shape=jax.ShapeDtypeStruct(kernel.shape, jnp.float32),
        in_specs=[whole()],
        out_specs=whole(),
        name="mirror_taps",
    )(summed)
    return (outputs, kernel_grad)


def solution(mesh):
    split = P(AXES, None, None, None)
    return jax.shard_map(
        per_device,
        mesh=mesh,
        in_specs=(split, split, P()),
        out_specs=(split, P()),
        check_vma=False,
    )
```

```python
import functools
import math

import jax
import jax.numpy as jnp
import numpy as np
from jax import lax
from jax.experimental import pallas as pl
from jax.experimental.pallas import tpu as pltpu
from jax.sharding import PartitionSpec as P

AXES = ("sample", "freq")
APPLICATIONS = 7
CHAINS = 2
IN_PARTS = 4
AHEAD = 2
UNROLL = 8
GROUPS = 2
HALF_TAPS = ((1, 1), (1, 2), (2, 0), (2, 1), (2, 2))
VMEM_LIMIT = 56 * 1024 * 1024


def split_table(table):
    high = table.astype(jnp.bfloat16)
    low = (table - high.astype(np.float64)).astype(jnp.bfloat16)
    return high, low


def forward_table(number, side):
    place = np.arange(side)
    table = np.zeros((side, side))
    table[0] = 1.0
    table[1] = np.cos(np.pi * place)
    for slot in range(1, side // 2):
        angle = 2.0 * math.pi * ((slot * place) % side) / side
        table[2 * slot] = np.cos(angle)
        table[2 * slot + 1] = -np.sin(angle)
    full = np.einsum("kw,nm->knmw", table, np.eye(number))
    return full.reshape(side * number, number * side)


def inverse_table(number, side):
    place = np.arange(side)
    table = np.zeros((side, side))
    table[:, 0] = 2.0 / side
    table[:, 1] = 2.0 / side * np.cos(np.pi * place)
    for slot in range(1, side // 2):
        angle = 2.0 * math.pi * ((slot * place) % side) / side
        table[:, 2 * slot] = 4.0 / side * np.cos(angle)
        table[:, 2 * slot + 1] = -4.0 / side * np.sin(angle)
    full = np.einsum("wk,nm->nwkm", table, np.eye(number))
    return full.reshape(number * side, side * number)


def slot_factors(side):
    rows = [[1.0, -1.0, 0.0, 1.0 / side]]
    for slot in range(1, side // 2):
        angle = 2.0 * math.pi * slot / side
        rows.append([math.cos(angle), math.cos(angle), math.sin(angle), 2.0 / side])
    table = np.array(rows)
    weighted = table[:, :3] * table[:, 3:]
    return np.concatenate([table, weighted], axis=1).astype(np.float32)


def dot(left, right):
    return jnp.dot(left, right, preferred_element_type=jnp.float32)


def main_kernel(
    scale,
    factor_ref,
    x_hbm,
    t_hbm,
    kernel_hbm,
    table_hbm,
    dev_hbm,
    grad_ref,
    x_ref,
    t_ref,
    kernel_ref,
    table_ref,
    base_ref,
    held_ref,
    weight_ref,
    taps_ref,
    sums_ref,
    dev_ref,
    left_ref,
    right_ref,
    in_sems,
    other_sems,
    out_sems,
):
    number, side, _, channels = x_ref.shape
    slots = side // 2
    wide = 2 * channels
    pairs = side // 2
    part = side // IN_PARTS

    def incoming(index, place):
        source, target = ((x_hbm, x_ref), (t_hbm, t_ref))[index]
        rows = pl.ds(place * part, part)
        return pltpu.make_async_copy(
            source.at[:, rows], target.at[:, rows], in_sems.at[index, place]
        )

    def outgoing(slot):
        return pltpu.make_async_copy(dev_ref.at[slot], dev_hbm.at[slot], out_sems.at[slot])

    table_copy = pltpu.make_async_copy(table_hbm, table_ref, other_sems.at[0])
    kernel_copy = pltpu.make_async_copy(kernel_hbm, kernel_ref, other_sems.at[1])
    table_copy.start()
    for place in range(AHEAD):
        for index in range(2):
            incoming(index, place).start()
    kernel_copy.start()
    sums_ref[...] = jnp.zeros_like(sums_ref)
    left_ref[...] = jnp.zeros_like(left_ref)
    right_ref[...] = jnp.zeros_like(right_ref)

    def make_taps():
        for a in range(3):
            flipped = [kernel_ref[a, b].T - kernel_ref[2 - a, 2 - b] for b in range(3)]
            place = 3 - 3 * a // 2 if a != 1 else 1
            taps_ref[place, 0] = -flipped[1]
            taps_ref[place, 1] = -(flipped[2] + flipped[0])
            taps_ref[place, 2] = flipped[2] - flipped[0]
        outside = 0.5 * (taps_ref[0] + taps_ref[3])
        inside = 0.5 * taps_ref[1]
        taps_ref[1] = outside + inside
        taps_ref[2] = outside - inside

    def transform(h, carry):
        rows = jnp.concatenate(
            [
                x_ref[:, h].reshape(number * side, channels),
                t_ref[:, h].reshape(number * side, channels),
            ],
            axis=1,
        )
        both = dot(table_ref[...], rows)
        half = side * number
        result = (both[:half] + both[half:]).reshape(slots, 2, number, wide)
        pair, odd = h // 2, h % 2
        base_ref[:, odd, pair, :number, :channels] = result[:, 0, :, :channels]
        base_ref[:, odd, pair, :number, channels:] = result[:, 1, :, :channels]
        base_ref[:, odd, pair, number:, :channels] = result[:, 0, :, channels:]
        base_ref[:, odd, pair, number:, channels:] = result[:, 1, :, channels:]
        return carry

    def before_of(rows):
        return jnp.concatenate([rows[pairs - 1 :], rows[: pairs - 1]], axis=0)

    def after_of(rows):
        return jnp.concatenate([rows[1:], rows[:1]], axis=0)

    def store_held(chain, parity, even, odd):
        held_ref[chain, parity, 0] = (before_of(odd) - odd).astype(jnp.bfloat16)
        held_ref[chain, parity, 1] = (even + odd).astype(jnp.bfloat16)
        held_ref[chain, parity, 2] = (odd - even).astype(jnp.bfloat16)
        held_ref[chain, parity, 3] = (even - after_of(even)).astype(jnp.bfloat16)

    def prepare_taps(buffer, slot, a):
        cos_top, cos_low, sine = (factor_ref[slot, j] for j in range(3))
        first, second = taps_ref[a, 0], taps_ref[a, 1]
        cross = (sine * taps_ref[a, 2]).astype(jnp.bfloat16)
        weight_ref[buffer, a, :channels, :channels] = (first + cos_top * second).astype(jnp.bfloat16)
        weight_ref[buffer, a, channels:, channels:] = (first + cos_low * second).astype(jnp.bfloat16)
        weight_ref[buffer, a, :channels, channels:] = cross
        weight_ref[buffer, a, channels:, :channels] = -cross

    def apply(buffer, chain, parity, slot):
        def part(place):
            left = held_ref[chain, parity, place].reshape(pairs * 2 * number, wide)
            return dot(left, weight_ref[buffer, place]).reshape(pairs, 2 * number, wide)

        first, inner, outer, last = (part(place) for place in range(4))
        return first + (inner + outer), (inner - outer) - last

    def advance(moved, base, step):
        x_new = base[:, :number] + moved[:, :number]
        if step % 2 == 0:
            t_new = moved[:, number:] - base[:, number:]
        else:
            t_new = moved[:, number:] + base[:, number:]
        return x_new, t_new

    def finish(buffer, slot, even, odd, even_new, odd_new):
        for place, moved in enumerate((even, odd)):
            dev_ref[slot, place, :, 0] = moved[:, :number, :channels]
            dev_ref[slot, place, :, 1] = moved[:, :number, channels:]
        half = pairs * number
        even_x, even_t = even_new
        odd_x, odd_t = odd_new
        left_ref[buffer, :half] = even_t.reshape(half, wide).astype(jnp.bfloat16)
        left_ref[buffer, half:] = odd_t.reshape(half, wide).astype(jnp.bfloat16)
        shifted = ((odd_x, after_of(even_x)), (even_x, odd_x), (before_of(odd_x), even_x))
        for a, (top, low) in enumerate(shifted):
            columns = slice(a * wide, (a + 1) * wide)
            right_ref[buffer, :half, columns] = top.reshape(half, wide).astype(jnp.bfloat16)
            right_ref[buffer, half:, columns] = low.reshape(half, wide).astype(jnp.bfloat16)

    def products(buffer, slot):
        weight, top, low, sine = (factor_ref[slot, j] for j in range(3, 7))
        outer_all = lax.dot_general(
            left_ref[buffer],
            right_ref[buffer],
            (((0,), (0,)), ((), ())),
            preferred_element_type=jnp.float32,
        )
        for a in range(3):
            outer = outer_all[:, a * wide : (a + 1) * wide]
            upper, lower = outer[:channels, :channels], outer[channels:, channels:]
            sums_ref[a, 0] += weight * (upper + lower)
            sums_ref[a, 1] += top * upper + low * lower
            sums_ref[a, 2] += sine * (outer[channels:, :channels] - outer[:channels, channels:])

    def work(group, odd):
        here, first = (CHAINS, 1) if odd else (0, 0)
        there = CHAINS - here
        before = jnp.maximum((group - 1) * CHAINS, 0)
        after = jnp.minimum((group + 1) * CHAINS, slots - CHAINS)
        jobs = [
            functools.partial(products, there + chain, before + chain) for chain in range(CHAINS)
        ] + [
            functools.partial(prepare_taps, there + chain, after + chain, a)
            for chain in range(CHAINS)
            for a in range(4)
        ]
        share = -(-len(jobs) // ((APPLICATIONS - 1) * CHAINS))
        for step in range(APPLICATIONS):
            for chain in range(CHAINS):
                slot = group * CHAINS + chain
                even, odd = apply(here + chain, chain, (first + step) % 2, slot)
                even_new = advance(even, base_ref[slot, 0], step)
                odd_new = advance(odd, base_ref[slot, 1], step)
                if step < APPLICATIONS - 1:
                    store_held(
                        chain,
                        (first + step + 1) % 2,
                        jnp.concatenate(even_new, axis=1),
                        jnp.concatenate(odd_new, axis=1),
                    )
                else:
                    finish(here + chain, slot, even, odd, even_new, odd_new)
                if step == APPLICATIONS - 2:
                    store_held(
                        chain, 1 - first, base_ref[after + chain, 0], base_ref[after + chain, 1]
                    )
                for job in jobs[:share]:
                    job()
                jobs = jobs[share:]

    table_copy.wait()
    for place in range(IN_PARTS):
        for index in range(2):
            incoming(index, place).wait()
        if place + AHEAD < IN_PARTS:
            for index in range(2):
                incoming(index, place + AHEAD).start()
        if place == 1:
            kernel_copy.wait()
            make_taps()
        lax.fori_loop(place * part, (place + 1) * part, transform, 0, unroll=UNROLL)
    for chain in range(CHAINS):
        for a in range(4):
            prepare_taps(chain, chain, a)
        store_held(chain, 0, base_ref[chain, 0], base_ref[chain, 1])

    def some_groups(index, carry):
        for member in range(GROUPS):
            work(GROUPS * index + member, member % 2 == 1)
        for slot in range(GROUPS * CHAINS):
            outgoing(index * GROUPS * CHAINS + slot).start()
        return carry

    lax.fori_loop(0, slots // (GROUPS * CHAINS), some_groups, 0)
    for chain in range(CHAINS):
        products(CHAINS + chain, slots - CHAINS + chain)

    def correlation(a, b):
        if b == 1:
            return sums_ref[a, 0]
        if b == 2:
            return sums_ref[a, 1] - sums_ref[a, 2]
        return sums_ref[a, 1] + sums_ref[a, 2]

    for place, (a, b) in enumerate(HALF_TAPS):
        piece = scale * (correlation(a, b) - correlation(2 - a, 2 - b).T)
        grad_ref[place * channels : (place + 1) * channels] = piece.astype(grad_ref.dtype)
    rows = len(HALF_TAPS) * channels
    if grad_ref.shape[0] > rows:
        grad_ref[rows:] = jnp.zeros((grad_ref.shape[0] - rows, channels), grad_ref.dtype)
    for slot in range(slots):
        outgoing(slot).wait()


def inverse_kernel(x_ref, dev_ref, high_ref, low_ref, out_ref):
    number, side, _, channels = x_ref.shape

    def transform(pair, carry):
        rows = jnp.concatenate(
            [dev_ref[:, j, pair].reshape(side * number, channels) for j in range(2)], axis=1
        )
        high = rows.astype(jnp.bfloat16)
        low = (rows - high.astype(jnp.float32)).astype(jnp.bfloat16)
        result = dot(high_ref[...], high) + dot(low_ref[...], high) + dot(high_ref[...], low)
        for j in range(2):
            h = 2 * pair + j
            piece = result[:, j * channels : (j + 1) * channels]
            piece = piece.reshape(number, side, channels) + x_ref[:, h].astype(jnp.float32)
            out_ref[:, h] = piece.astype(jnp.bfloat16)
        return carry

    lax.fori_loop(0, side // 2, transform, 0, unroll=2)


def mirror_kernel(sum_ref, grad_ref):
    channels = sum_ref.shape[1]
    for place, (a, b) in enumerate(HALF_TAPS):
        piece = sum_ref[place * channels : (place + 1) * channels].astype(jnp.float32)
        grad_ref[a, b] = piece
        if place:
            grad_ref[2 - a, 2 - b] = -piece.T


def whole(memory_space=pltpu.VMEM):
    return pl.BlockSpec(memory_space=memory_space)


def device_sum(partial, count):
    terms = lax.all_to_all(
        partial.reshape(count, -1, partial.shape[1]), AXES, split_axis=0, concat_axis=0, tiled=True
    )
    own = jnp.sum(terms.astype(jnp.float32), axis=0, keepdims=True).astype(partial.dtype)
    shares = lax.all_to_all(
        jnp.broadcast_to(own, terms.shape), AXES, split_axis=0, concat_axis=0, tiled=True
    )
    return shares.reshape(partial.shape)


def per_device(images, cotangent, kernel):
    number, side, _, channels = images.shape
    slots = side // 2
    wide = 2 * channels
    count = lax.axis_size("sample") * lax.axis_size("freq")
    share = -(-len(HALF_TAPS) * channels // (8 * count)) * 8
    forward_both = np.concatenate(split_table(forward_table(number, side)), axis=0)
    inverse_high, inverse_low = split_table(inverse_table(number, side))
    rows = side * 2 * number
    params = pltpu.CompilerParams(vmem_limit_bytes=VMEM_LIMIT)
    deviation, partial = pl.pallas_call(
        functools.partial(main_kernel, 2.0 / (number * count)),
        out_shape=(
            jax.ShapeDtypeStruct((slots, 2, side // 2, 2, number, channels), jnp.float32),
            jax.ShapeDtypeStruct((count * share, channels), jnp.bfloat16),
        ),
        in_specs=[whole(pltpu.SMEM)] + [whole(pl.ANY)] * 4,
        out_specs=(whole(pl.ANY), whole()),
        scratch_shapes=[
            pltpu.VMEM(images.shape, jnp.bfloat16),
            pltpu.VMEM(images.shape, jnp.bfloat16),
            pltpu.VMEM(kernel.shape, jnp.float32),
            pltpu.VMEM(forward_both.shape, jnp.bfloat16),
            pltpu.VMEM((slots, 2, side // 2, 2 * number, wide), jnp.float32),
            pltpu.VMEM((CHAINS, 2, 4, side // 2, 2 * number, wide), jnp.bfloat16),
            pltpu.VMEM((2 * CHAINS, 4, wide, wide), jnp.bfloat16),
            pltpu.VMEM((4, 3, channels, channels), jnp.float32),
            pltpu.VMEM((3, 3, channels, channels), jnp.float32),
            pltpu.VMEM((slots, 2, side // 2, 2, number, channels), jnp.float32),
            pltpu.VMEM((2 * CHAINS, side * number, wide), jnp.bfloat16),
            pltpu.VMEM((2 * CHAINS, side * number, 3 * wide), jnp.bfloat16),
            pltpu.SemaphoreType.DMA((2, IN_PARTS)),
            pltpu.SemaphoreType.DMA((2,)),
            pltpu.SemaphoreType.DMA((slots,)),
        ],
        compiler_params=params,
        cost_estimate=pl.CostEstimate(
            flops=2 * APPLICATIONS * slots * rows * 3 * wide * wide,
            bytes_accessed=12 * 1024 * 1024,
            transcendentals=0,
        ),
        name="horner_and_gradient",
    )(
        jnp.asarray(slot_factors(side)),
        images,
        cotangent,
        kernel,
        jnp.asarray(forward_both),
    )
    summed = device_sum(partial, count)
    outputs = pl.pallas_call(
        inverse_kernel,
        out_shape=jax.ShapeDtypeStruct(images.shape, jnp.bfloat16),
        in_specs=[whole()] * 4,
        out_specs=whole(),
        compiler_params=params,
        cost_estimate=pl.CostEstimate(
            flops=6 * side * side * number * side * number * channels,
            bytes_accessed=8 * 1024 * 1024,
            transcendentals=0,
        ),
        name="inverse_transform",
    )(images, deviation, jnp.asarray(inverse_high), jnp.asarray(inverse_low))
    kernel_grad = pl.pallas_call(
        mirror_kernel,
        out_shape=jax.ShapeDtypeStruct(kernel.shape, jnp.float32),
        in_specs=[whole()],
        out_specs=whole(),
        name="mirror_taps",
    )(summed)
    return (outputs, kernel_grad)


def solution(mesh):
    split = P(AXES, None, None, None)
    return jax.shard_map(
        per_device,
        mesh=mesh,
        in_specs=(split, split, P()),
        out_specs=(split, P()),
        check_vma=False,
    )
```

```python
import functools
import math

import jax
import jax.numpy as jnp
import numpy as np
from jax import lax
from jax.experimental import pallas as pl
from jax.experimental.pallas import tpu as pltpu
from jax.sharding import PartitionSpec as P

AXES = ("sample", "freq")
APPLICATIONS = 7
CHAINS = 2
IN_PARTS = 4
AHEAD = 2
UNROLL = 8
GROUPS = 2
HALF_TAPS = ((1, 1), (1, 2), (2, 0), (2, 1), (2, 2))
VMEM_LIMIT = 56 * 1024 * 1024
MIRROR_LIMIT = 4 * 1024 * 1024


def split_table(table):
    high = table.astype(jnp.bfloat16)
    low = (table - high.astype(np.float64)).astype(jnp.bfloat16)
    return high, low


def forward_table(number, side):
    place = np.arange(side)
    table = np.zeros((side, side))
    table[0] = 1.0
    table[1] = np.cos(np.pi * place)
    for slot in range(1, side // 2):
        angle = 2.0 * math.pi * ((slot * place) % side) / side
        table[2 * slot] = np.cos(angle)
        table[2 * slot + 1] = -np.sin(angle)
    full = np.einsum("kw,nm->knmw", table, np.eye(number))
    return full.reshape(side * number, number * side)


def inverse_table(number, side):
    place = np.arange(side)
    table = np.zeros((side, side))
    table[:, 0] = 2.0 / side
    table[:, 1] = 2.0 / side * np.cos(np.pi * place)
    for slot in range(1, side // 2):
        angle = 2.0 * math.pi * ((slot * place) % side) / side
        table[:, 2 * slot] = 4.0 / side * np.cos(angle)
        table[:, 2 * slot + 1] = -4.0 / side * np.sin(angle)
    full = np.einsum("wk,nm->nwkm", table, np.eye(number))
    return full.reshape(number * side, side * number)


def slot_factors(side):
    rows = [[1.0, -1.0, 0.0, 1.0 / side]]
    for slot in range(1, side // 2):
        angle = 2.0 * math.pi * slot / side
        rows.append([math.cos(angle), math.cos(angle), math.sin(angle), 2.0 / side])
    table = np.array(rows)
    weighted = table[:, :3] * table[:, 3:]
    return np.concatenate([table, weighted], axis=1).astype(np.float32)


def dot(left, right):
    return jnp.dot(left, right, preferred_element_type=jnp.float32)


def main_kernel(
    factor_ref,
    x_hbm,
    t_hbm,
    kernel_hbm,
    table_hbm,
    dev_hbm,
    grad_ref,
    x_ref,
    t_ref,
    kernel_ref,
    table_ref,
    base_ref,
    held_ref,
    weight_ref,
    taps_ref,
    sums_ref,
    dev_ref,
    left_ref,
    right_ref,
    in_sems,
    other_sems,
    out_sems,
):
    number, side, _, channels = x_ref.shape
    slots = side // 2
    wide = 2 * channels
    pairs = side // 2
    part = side // IN_PARTS

    def incoming(index, place):
        source, target = ((x_hbm, x_ref), (t_hbm, t_ref))[index]
        rows = pl.ds(place * part, part)
        return pltpu.make_async_copy(
            source.at[:, rows], target.at[:, rows], in_sems.at[index, place]
        )

    def outgoing(slot):
        return pltpu.make_async_copy(dev_ref.at[slot], dev_hbm.at[slot], out_sems.at[slot])

    table_copy = pltpu.make_async_copy(table_hbm, table_ref, other_sems.at[0])
    kernel_copy = pltpu.make_async_copy(kernel_hbm, kernel_ref, other_sems.at[1])
    table_copy.start()
    for place in range(AHEAD):
        for index in range(2):
            incoming(index, place).start()
    kernel_copy.start()
    sums_ref[...] = jnp.zeros_like(sums_ref)
    left_ref[...] = jnp.zeros_like(left_ref)
    right_ref[...] = jnp.zeros_like(right_ref)

    def make_taps():
        for a in range(3):
            flipped = [kernel_ref[a, b].T - kernel_ref[2 - a, 2 - b] for b in range(3)]
            place = 3 - 3 * a // 2 if a != 1 else 1
            taps_ref[place, 0] = -flipped[1]
            taps_ref[place, 1] = -(flipped[2] + flipped[0])
            taps_ref[place, 2] = flipped[2] - flipped[0]
        outside = 0.5 * (taps_ref[0] + taps_ref[3])
        inside = 0.5 * taps_ref[1]
        taps_ref[1] = outside + inside
        taps_ref[2] = outside - inside

    def transform(h, carry):
        rows = jnp.concatenate(
            [
                x_ref[:, h].reshape(number * side, channels),
                t_ref[:, h].reshape(number * side, channels),
            ],
            axis=1,
        )
        both = dot(table_ref[...], rows)
        half = side * number
        result = (both[:half] + both[half:]).reshape(slots, 2, number, wide)
        pair, odd = h // 2, h % 2
        base_ref[:, odd, pair, :number, :channels] = result[:, 0, :, :channels]
        base_ref[:, odd, pair, :number, channels:] = result[:, 1, :, :channels]
        base_ref[:, odd, pair, number:, :channels] = result[:, 0, :, channels:]
        base_ref[:, odd, pair, number:, channels:] = result[:, 1, :, channels:]
        return carry

    def before_of(rows):
        return jnp.concatenate([rows[pairs - 1 :], rows[: pairs - 1]], axis=0)

    def after_of(rows):
        return jnp.concatenate([rows[1:], rows[:1]], axis=0)

    def store_held(chain, parity, even, odd):
        even, odd = even.astype(jnp.bfloat16), odd.astype(jnp.bfloat16)
        held_ref[chain, parity, 0] = before_of(odd) - odd
        held_ref[chain, parity, 1] = even + odd
        held_ref[chain, parity, 2] = odd - even
        held_ref[chain, parity, 3] = even - after_of(even)

    def prepare_taps(buffer, slot, a):
        cos_top, cos_low, sine = (factor_ref[slot, j] for j in range(3))
        first, second = taps_ref[a, 0], taps_ref[a, 1]
        cross = (sine * taps_ref[a, 2]).astype(jnp.bfloat16)
        weight_ref[buffer, a, :channels, :channels] = (first + cos_top * second).astype(jnp.bfloat16)
        weight_ref[buffer, a, channels:, channels:] = (first + cos_low * second).astype(jnp.bfloat16)
        weight_ref[buffer, a, :channels, channels:] = cross
        weight_ref[buffer, a, channels:, :channels] = -cross

    def apply(buffer, chain, parity, slot):
        def part(place):
            left = held_ref[chain, parity, place].reshape(pairs * 2 * number, wide)
            return dot(left, weight_ref[buffer, place]).reshape(pairs, 2 * number, wide)

        first, inner, outer, last = (part(place) for place in range(4))
        return first + (inner + outer), (inner - outer) - last

    def advance(moved, base, step):
        x_new = base[:, :number] + moved[:, :number]
        if step % 2 == 0:
            t_new = moved[:, number:] - base[:, number:]
        else:
            t_new = moved[:, number:] + base[:, number:]
        return x_new, t_new

    def finish(buffer, slot, even, odd, even_new, odd_new):
        for place, moved in enumerate((even, odd)):
            dev_ref[slot, place, :, 0] = moved[:, :number, :channels]
            dev_ref[slot, place, :, 1] = moved[:, :number, channels:]
        half = pairs * number
        even_x, even_t = even_new
        odd_x, odd_t = odd_new
        left_ref[buffer, :half] = even_t.reshape(half, wide).astype(jnp.bfloat16)
        left_ref[buffer, half:] = odd_t.reshape(half, wide).astype(jnp.bfloat16)
        shifted = ((odd_x, after_of(even_x)), (even_x, odd_x), (before_of(odd_x), even_x))
        for a, (top, low) in enumerate(shifted):
            columns = slice(a * wide, (a + 1) * wide)
            right_ref[buffer, :half, columns] = top.reshape(half, wide).astype(jnp.bfloat16)
            right_ref[buffer, half:, columns] = low.reshape(half, wide).astype(jnp.bfloat16)

    def products(buffer, slot):
        weight, top, low, sine = (factor_ref[slot, j] for j in range(3, 7))
        outer_all = lax.dot_general(
            left_ref[buffer],
            right_ref[buffer],
            (((0,), (0,)), ((), ())),
            preferred_element_type=jnp.float32,
        )
        for a in range(3):
            outer = outer_all[:, a * wide : (a + 1) * wide]
            upper, lower = outer[:channels, :channels], outer[channels:, channels:]
            sums_ref[a, 0] += weight * (upper + lower)
            sums_ref[a, 1] += top * upper + low * lower
            sums_ref[a, 2] += sine * (outer[channels:, :channels] - outer[:channels, channels:])

    def work(group, odd):
        here, first = (CHAINS, 1) if odd else (0, 0)
        there = CHAINS - here
        before = jnp.maximum((group - 1) * CHAINS, 0)
        after = jnp.minimum((group + 1) * CHAINS, slots - CHAINS)
        jobs = [
            functools.partial(products, there + chain, before + chain) for chain in range(CHAINS)
        ] + [
            functools.partial(prepare_taps, there + chain, after + chain, a)
            for chain in range(CHAINS)
            for a in range(4)
        ]
        share = -(-len(jobs) // ((APPLICATIONS - 1) * CHAINS))
        for step in range(APPLICATIONS):
            for chain in range(CHAINS):
                slot = group * CHAINS + chain
                even, odd = apply(here + chain, chain, (first + step) % 2, slot)
                even_new = advance(even, base_ref[slot, 0], step)
                odd_new = advance(odd, base_ref[slot, 1], step)
                if step < APPLICATIONS - 1:
                    store_held(
                        chain,
                        (first + step + 1) % 2,
                        jnp.concatenate(even_new, axis=1),
                        jnp.concatenate(odd_new, axis=1),
                    )
                else:
                    finish(here + chain, slot, even, odd, even_new, odd_new)
                if step == APPLICATIONS - 2:
                    store_held(
                        chain, 1 - first, base_ref[after + chain, 0], base_ref[after + chain, 1]
                    )
                for job in jobs[:share]:
                    job()
                jobs = jobs[share:]

    table_copy.wait()
    for place in range(IN_PARTS):
        for index in range(2):
            incoming(index, place).wait()
        if place + AHEAD < IN_PARTS:
            for index in range(2):
                incoming(index, place + AHEAD).start()
        if place == 1:
            kernel_copy.wait()
            make_taps()
            for chain in range(CHAINS):
                for a in range(4):
                    prepare_taps(chain, chain, a)
        lax.fori_loop(place * part, (place + 1) * part, transform, 0, unroll=UNROLL)
    for chain in range(CHAINS):
        store_held(chain, 0, base_ref[chain, 0], base_ref[chain, 1])

    def some_groups(index, carry):
        for member in range(GROUPS):
            work(GROUPS * index + member, member % 2 == 1)
        for slot in range(GROUPS * CHAINS):
            outgoing(index * GROUPS * CHAINS + slot).start()
        return carry

    lax.fori_loop(0, slots // (GROUPS * CHAINS), some_groups, 0)
    for chain in range(CHAINS):
        products(CHAINS + chain, slots - CHAINS + chain)

    def correlation(a, b):
        if b == 1:
            return sums_ref[a, 0]
        if b == 2:
            return sums_ref[a, 1] - sums_ref[a, 2]
        return sums_ref[a, 1] + sums_ref[a, 2]

    for place, (a, b) in enumerate(HALF_TAPS):
        piece = correlation(a, b) - correlation(2 - a, 2 - b).T
        grad_ref[place * channels : (place + 1) * channels] = piece.astype(grad_ref.dtype)
    rows = len(HALF_TAPS) * channels
    if grad_ref.shape[0] > rows:
        grad_ref[rows:] = jnp.zeros((grad_ref.shape[0] - rows, channels), grad_ref.dtype)
    for slot in range(slots):
        outgoing(slot).wait()


def inverse_kernel(x_ref, dev_ref, high_ref, low_ref, out_ref):
    number, side, _, channels = x_ref.shape

    def transform(pair, carry):
        rows = jnp.concatenate(
            [dev_ref[:, j, pair].reshape(side * number, channels) for j in range(2)], axis=1
        )
        high = rows.astype(jnp.bfloat16)
        low = (rows - high.astype(jnp.float32)).astype(jnp.bfloat16)
        result = dot(high_ref[...], high) + dot(low_ref[...], high) + dot(high_ref[...], low)
        for j in range(2):
            h = 2 * pair + j
            piece = result[:, j * channels : (j + 1) * channels]
            piece = piece.reshape(number, side, channels) + x_ref[:, h].astype(jnp.float32)
            out_ref[:, h] = piece.astype(jnp.bfloat16)
        return carry

    lax.fori_loop(0, side // 2, transform, 0, unroll=2)


def mirror_kernel(sum_ref, grad_ref):
    channels = sum_ref.shape[1]
    for place, (a, b) in enumerate(HALF_TAPS):
        piece = sum_ref[place * channels : (place + 1) * channels].astype(jnp.float32)
        grad_ref[a, b] = piece
        if place:
            grad_ref[2 - a, 2 - b] = -piece.T


def whole(memory_space=pltpu.VMEM):
    return pl.BlockSpec(memory_space=memory_space)


def device_sum(partial, scale, count):
    pieces = partial.reshape(count, -1, 2, partial.shape[1])
    terms = lax.all_to_all(pieces, AXES, split_axis=0, concat_axis=0, tiled=True)
    own = jnp.sum(scale * terms.astype(jnp.float32), axis=0, keepdims=True).astype(partial.dtype)
    shares = lax.all_to_all(
        jnp.broadcast_to(own, terms.shape), AXES, split_axis=0, concat_axis=0, tiled=True
    )
    return shares.reshape(partial.shape)


def per_device(images, cotangent, kernel):
    number, side, _, channels = images.shape
    slots = side // 2
    wide = 2 * channels
    count = lax.axis_size("sample") * lax.axis_size("freq")
    share = -(-len(HALF_TAPS) * channels // (2 * count)) * 2
    forward_both = np.concatenate(split_table(forward_table(number, side)), axis=0)
    inverse_high, inverse_low = split_table(inverse_table(number, side))
    rows = side * 2 * number
    params = pltpu.CompilerParams(vmem_limit_bytes=VMEM_LIMIT)
    deviation, partial = pl.pallas_call(
        main_kernel,
        out_shape=(
            jax.ShapeDtypeStruct((slots, 2, side // 2, 2, number, channels), jnp.float32),
            jax.ShapeDtypeStruct((count * share, channels), jnp.bfloat16),
        ),
        in_specs=[whole(pltpu.SMEM)] + [whole(pl.ANY)] * 4,
        out_specs=(whole(pl.ANY), whole()),
        scratch_shapes=[
            pltpu.VMEM(images.shape, jnp.bfloat16),
            pltpu.VMEM(images.shape, jnp.bfloat16),
            pltpu.VMEM(kernel.shape, jnp.float32),
            pltpu.VMEM(forward_both.shape, jnp.bfloat16),
            pltpu.VMEM((slots, 2, side // 2, 2 * number, wide), jnp.float32),
            pltpu.VMEM((CHAINS, 2, 4, side // 2, 2 * number, wide), jnp.bfloat16),
            pltpu.VMEM((2 * CHAINS, 4, wide, wide), jnp.bfloat16),
            pltpu.VMEM((4, 3, channels, channels), jnp.float32),
            pltpu.VMEM((3, 3, channels, channels), jnp.float32),
            pltpu.VMEM((slots, 2, side // 2, 2, number, channels), jnp.float32),
            pltpu.VMEM((2 * CHAINS, side * number, wide), jnp.bfloat16),
            pltpu.VMEM((2 * CHAINS, side * number, 3 * wide), jnp.bfloat16),
            pltpu.SemaphoreType.DMA((2, IN_PARTS)),
            pltpu.SemaphoreType.DMA((2,)),
            pltpu.SemaphoreType.DMA((slots,)),
        ],
        compiler_params=params,
        cost_estimate=pl.CostEstimate(
            flops=2 * APPLICATIONS * slots * rows * 3 * wide * wide,
            bytes_accessed=12 * 1024 * 1024,
            transcendentals=0,
        ),
        name="horner_and_gradient",
    )(
        jnp.asarray(slot_factors(side)),
        images,
        cotangent,
        kernel,
        jnp.asarray(forward_both),
    )
    summed = device_sum(partial, 2.0 / (number * count), count)
    outputs = pl.pallas_call(
        inverse_kernel,
        out_shape=jax.ShapeDtypeStruct(images.shape, jnp.bfloat16),
        in_specs=[whole()] * 4,
        out_specs=whole(),
        compiler_params=params,
        cost_estimate=pl.CostEstimate(
            flops=6 * side * side * number * side * number * channels,
            bytes_accessed=8 * 1024 * 1024,
            transcendentals=0,
        ),
        name="inverse_transform",
    )(images, deviation, jnp.asarray(inverse_high), jnp.asarray(inverse_low))
    kernel_grad = pl.pallas_call(
        mirror_kernel,
        out_shape=jax.ShapeDtypeStruct(kernel.shape, jnp.float32),
        in_specs=[whole()],
        out_specs=whole(),
        compiler_params=pltpu.CompilerParams(vmem_limit_bytes=MIRROR_LIMIT),
        name="mirror_taps",
    )(summed)
    return (outputs, kernel_grad)


def solution(mesh):
    split = P(AXES, None, None, None)
    return jax.shard_map(
        per_device,
        mesh=mesh,
        in_specs=(split, split, P()),
        out_specs=(split, P()),
        check_vma=False,
    )
```

```python
import functools
import math

import jax
import jax.numpy as jnp
import numpy as np
from jax import lax
from jax.experimental import pallas as pl
from jax.experimental.pallas import tpu as pltpu
from jax.sharding import PartitionSpec as P

AXES = ("sample", "freq")
APPLICATIONS = 7
CHAINS = 2
IN_PARTS = 4
AHEAD = 2
LAG = 0
GROUPS = 2
HALF_TAPS = ((1, 1), (1, 2), (2, 0), (2, 1), (2, 2))
VMEM_LIMIT = 56 * 1024 * 1024
MIRROR_LIMIT = 4 * 1024 * 1024


def split_table(table):
    high = table.astype(jnp.bfloat16)
    low = (table - high.astype(np.float64)).astype(jnp.bfloat16)
    return high, low


def forward_table(number, side):
    place = np.arange(side)
    table = np.zeros((side, side))
    table[0] = 1.0
    table[1] = np.cos(np.pi * place)
    for slot in range(1, side // 2):
        angle = 2.0 * math.pi * ((slot * place) % side) / side
        table[2 * slot] = np.cos(angle)
        table[2 * slot + 1] = -np.sin(angle)
    full = np.einsum("kw,nm->knmw", table, np.eye(number))
    return full.reshape(side * number, number * side)


def inverse_table(number, side):
    place = np.arange(side)
    table = np.zeros((side, side))
    table[:, 0] = 2.0 / side
    table[:, 1] = 2.0 / side * np.cos(np.pi * place)
    for slot in range(1, side // 2):
        angle = 2.0 * math.pi * ((slot * place) % side) / side
        table[:, 2 * slot] = 4.0 / side * np.cos(angle)
        table[:, 2 * slot + 1] = -4.0 / side * np.sin(angle)
    full = np.einsum("wk,nm->nwkm", table, np.eye(number))
    return full.reshape(number * side, side * number)


def slot_factors(side):
    rows = [[1.0, -1.0, 0.0, 1.0 / side]]
    for slot in range(1, side // 2):
        angle = 2.0 * math.pi * slot / side
        rows.append([math.cos(angle), math.cos(angle), math.sin(angle), 2.0 / side])
    table = np.array(rows)
    weighted = table[:, :3] * table[:, 3:]
    return np.concatenate([table, weighted], axis=1).astype(np.float32)


def dot(left, right):
    return jnp.dot(left, right, preferred_element_type=jnp.float32)


def main_kernel(
    factor_ref,
    x_hbm,
    t_hbm,
    kernel_hbm,
    table_hbm,
    dev_hbm,
    grad_ref,
    x_ref,
    t_ref,
    kernel_ref,
    table_ref,
    base_ref,
    held_ref,
    weight_ref,
    taps_ref,
    sums_ref,
    dev_ref,
    left_ref,
    right_ref,
    in_sems,
    other_sems,
    out_sems,
):
    number, side, _, channels = x_ref.shape
    slots = side // 2
    wide = 2 * channels
    pairs = side // 2
    part = side // IN_PARTS

    def incoming(index, place):
        source, target = ((x_hbm, x_ref), (t_hbm, t_ref))[index]
        rows = pl.ds(place * part, part)
        return pltpu.make_async_copy(
            source.at[:, rows], target.at[:, rows], in_sems.at[index, place]
        )

    def outgoing(slot):
        return pltpu.make_async_copy(dev_ref.at[slot], dev_hbm.at[slot], out_sems.at[slot])

    table_copy = pltpu.make_async_copy(table_hbm, table_ref, other_sems.at[0])
    kernel_copy = pltpu.make_async_copy(kernel_hbm, kernel_ref, other_sems.at[1])
    table_copy.start()
    for place in range(AHEAD):
        for index in range(2):
            incoming(index, place).start()
        if place == 0:
            kernel_copy.start()
    def make_taps():
        for a in range(3):
            flipped = [kernel_ref[a, b].T - kernel_ref[2 - a, 2 - b] for b in range(3)]
            place = 3 - 3 * a // 2 if a != 1 else 1
            taps_ref[place, 0] = -flipped[1]
            taps_ref[place, 1] = -(flipped[2] + flipped[0])
            taps_ref[place, 2] = flipped[2] - flipped[0]
        outside = 0.5 * (taps_ref[0] + taps_ref[3])
        inside = 0.5 * taps_ref[1]
        taps_ref[1] = outside + inside
        taps_ref[2] = outside - inside

    def transform(h):
        rows = jnp.concatenate(
            [
                x_ref[:, h].reshape(number * side, channels),
                t_ref[:, h].reshape(number * side, channels),
            ],
            axis=1,
        )
        both = dot(table_ref[...], rows)
        half = side * number
        result = (both[:half] + both[half:]).reshape(slots, 2, number, wide)
        pair, odd = h // 2, h % 2
        base_ref[:, odd, pair, :number, :channels] = result[:, 0, :, :channels]
        base_ref[:, odd, pair, :number, channels:] = result[:, 1, :, :channels]
        base_ref[:, odd, pair, number:, :channels] = result[:, 0, :, channels:]
        base_ref[:, odd, pair, number:, channels:] = result[:, 1, :, channels:]

    def before_of(rows):
        return jnp.concatenate([rows[pairs - 1 :], rows[: pairs - 1]], axis=0)

    def after_of(rows):
        return jnp.concatenate([rows[1:], rows[:1]], axis=0)

    def store_held(chain, parity, even, odd):
        even, odd = even.astype(jnp.bfloat16), odd.astype(jnp.bfloat16)
        held_ref[chain, parity, 0] = before_of(odd) - odd
        held_ref[chain, parity, 1] = even + odd
        held_ref[chain, parity, 2] = odd - even
        held_ref[chain, parity, 3] = even - after_of(even)

    def prepare_taps(slot, a):
        cos_top, cos_low, sine = (factor_ref[slot, j] for j in range(3))
        first, second = taps_ref[a, 0], taps_ref[a, 1]
        cross = (sine * taps_ref[a, 2]).astype(jnp.bfloat16)
        top = (first + cos_top * second).astype(jnp.bfloat16)
        low = top if slot else (first + cos_low * second).astype(jnp.bfloat16)
        weight_ref[slot, a, :channels, :channels] = top
        weight_ref[slot, a, channels:, channels:] = low
        weight_ref[slot, a, :channels, channels:] = cross
        weight_ref[slot, a, channels:, :channels] = -cross

    def apply(chain, parity, slot):
        def part(place):
            left = held_ref[chain, parity, place].reshape(pairs * 2 * number, wide)
            return dot(left, weight_ref[slot, place]).reshape(pairs, 2 * number, wide)

        first, inner, outer, last = (part(place) for place in range(4))
        return first + (inner + outer), (inner - outer) - last

    def advance(moved, base, step):
        x_new = base[:, :number] + moved[:, :number]
        if step % 2 == 0:
            t_new = moved[:, number:] - base[:, number:]
        else:
            t_new = moved[:, number:] + base[:, number:]
        return x_new, t_new

    def finish(buffer, slot, even, odd, even_new, odd_new):
        for place, moved in enumerate((even, odd)):
            dev_ref[slot, place, :, 0] = moved[:, :number, :channels]
            dev_ref[slot, place, :, 1] = moved[:, :number, channels:]
        half = pairs * number
        even_x, even_t = even_new
        odd_x, odd_t = odd_new
        left_ref[buffer, :half] = even_t.reshape(half, wide).astype(jnp.bfloat16)
        left_ref[buffer, half:] = odd_t.reshape(half, wide).astype(jnp.bfloat16)
        shifted = ((odd_x, after_of(even_x)), (even_x, odd_x), (before_of(odd_x), even_x))
        for a, (top, low) in enumerate(shifted):
            columns = slice(a * wide, (a + 1) * wide)
            right_ref[buffer, :half, columns] = top.reshape(half, wide).astype(jnp.bfloat16)
            right_ref[buffer, half:, columns] = low.reshape(half, wide).astype(jnp.bfloat16)

    def products(buffer, slot):
        weight, top, low, sine = (factor_ref[slot, j] for j in range(3, 7))
        outer_all = lax.dot_general(
            left_ref[buffer],
            right_ref[buffer],
            (((0,), (0,)), ((), ())),
            preferred_element_type=jnp.float32,
        )
        for a in range(3):
            outer = outer_all[:, a * wide : (a + 1) * wide]
            upper, lower = outer[:channels, :channels], outer[channels:, channels:]
            sums_ref[a, 0] += weight * (upper + lower)
            sums_ref[a, 1] += top * upper + low * lower
            sums_ref[a, 2] += sine * (outer[channels:, :channels] - outer[:channels, channels:])

    def work(group, odd):
        here, first = (CHAINS, 1) if odd else (0, 0)
        there = CHAINS - here
        before = jnp.maximum((group - 1) * CHAINS, 0)
        after = jnp.minimum((group + 1) * CHAINS, slots - CHAINS)
        for step in range(APPLICATIONS):
            for chain in range(CHAINS):
                slot = group * CHAINS + chain
                even, odd = apply(chain, (first + step) % 2, slot)
                even_new = advance(even, base_ref[slot, 0], step)
                odd_new = advance(odd, base_ref[slot, 1], step)
                if step < APPLICATIONS - 1:
                    store_held(
                        chain,
                        (first + step + 1) % 2,
                        jnp.concatenate(even_new, axis=1),
                        jnp.concatenate(odd_new, axis=1),
                    )
                else:
                    finish(here + chain, slot, even, odd, even_new, odd_new)
                if step == APPLICATIONS - 2:
                    store_held(
                        chain, 1 - first, base_ref[after + chain, 0], base_ref[after + chain, 1]
                    )
                if step == LAG:
                    products(there + chain, before + chain)

    sums_ref[...] = jnp.zeros_like(sums_ref)
    left_ref[CHAINS:] = jnp.zeros_like(left_ref[CHAINS:])
    right_ref[CHAINS:] = jnp.zeros_like(right_ref[CHAINS:])
    jobs = [(slot, a) for slot in range(slots) for a in range(4)]
    table_copy.wait()
    for place in range(IN_PARTS):
        for index in range(2):
            incoming(index, place).wait()
        if place + AHEAD < IN_PARTS:
            for index in range(2):
                incoming(index, place + AHEAD).start()
        if place == 1:
            kernel_copy.wait()
            make_taps()
        for h in range(place * part, (place + 1) * part):
            transform(h)
            if place:
                turn, turns = h - part, side - part
                for job in jobs[turn * len(jobs) // turns : (turn + 1) * len(jobs) // turns]:
                    prepare_taps(*job)
    for chain in range(CHAINS):
        store_held(chain, 0, base_ref[chain, 0], base_ref[chain, 1])

    def some_groups(index, carry):
        for member in range(GROUPS):
            work(GROUPS * index + member, member % 2 == 1)
            for chain in range(CHAINS):
                outgoing((index * GROUPS + member) * CHAINS + chain).start()
        return carry

    lax.fori_loop(0, slots // (GROUPS * CHAINS), some_groups, 0)
    for chain in range(CHAINS):
        products(CHAINS + chain, slots - CHAINS + chain)

    def correlation(a, b):
        if b == 1:
            return sums_ref[a, 0]
        if b == 2:
            return sums_ref[a, 1] - sums_ref[a, 2]
        return sums_ref[a, 1] + sums_ref[a, 2]

    for place, (a, b) in enumerate(HALF_TAPS):
        piece = correlation(a, b) - correlation(2 - a, 2 - b).T
        grad_ref[place * channels : (place + 1) * channels] = piece.astype(grad_ref.dtype)
    rows = len(HALF_TAPS) * channels
    if grad_ref.shape[0] > rows:
        grad_ref[rows:] = jnp.zeros((grad_ref.shape[0] - rows, channels), grad_ref.dtype)
    for slot in range(slots):
        outgoing(slot).wait()


def inverse_kernel(x_ref, dev_ref, high_ref, low_ref, out_ref):
    number, side, _, channels = x_ref.shape

    def transform(pair, carry):
        rows = jnp.concatenate(
            [dev_ref[:, j, pair].reshape(side * number, channels) for j in range(2)], axis=1
        )
        high = rows.astype(jnp.bfloat16)
        low = (rows - high.astype(jnp.float32)).astype(jnp.bfloat16)
        result = dot(high_ref[...], high) + dot(low_ref[...], high) + dot(high_ref[...], low)
        for j in range(2):
            h = 2 * pair + j
            piece = result[:, j * channels : (j + 1) * channels]
            piece = piece.reshape(number, side, channels) + x_ref[:, h].astype(jnp.float32)
            out_ref[:, h] = piece.astype(jnp.bfloat16)
        return carry

    lax.fori_loop(0, side // 2, transform, 0, unroll=2)


def mirror_kernel(sum_ref, grad_ref):
    channels = sum_ref.shape[1]
    for place, (a, b) in enumerate(HALF_TAPS):
        piece = sum_ref[place * channels : (place + 1) * channels].astype(jnp.float32)
        grad_ref[a, b] = piece
        if place:
            grad_ref[2 - a, 2 - b] = -piece.T


def whole(memory_space=pltpu.VMEM):
    return pl.BlockSpec(memory_space=memory_space)


def device_sum(partial, scale, count):
    pieces = partial.reshape(count, -1, 2, partial.shape[1])
    terms = lax.all_to_all(pieces, AXES, split_axis=0, concat_axis=0, tiled=True)
    own = jnp.sum(scale * terms.astype(jnp.float32), axis=0, keepdims=True).astype(partial.dtype)
    shares = lax.all_to_all(
        jnp.broadcast_to(own, terms.shape), AXES, split_axis=0, concat_axis=0, tiled=True
    )
    return shares.reshape(partial.shape)


def per_device(images, cotangent, kernel):
    number, side, _, channels = images.shape
    slots = side // 2
    wide = 2 * channels
    count = lax.axis_size("sample") * lax.axis_size("freq")
    share = -(-len(HALF_TAPS) * channels // (2 * count)) * 2
    forward_both = np.concatenate(split_table(forward_table(number, side)), axis=0)
    inverse_high, inverse_low = split_table(inverse_table(number, side))
    rows = side * 2 * number
    params = pltpu.CompilerParams(vmem_limit_bytes=VMEM_LIMIT)
    deviation, partial = pl.pallas_call(
        main_kernel,
        out_shape=(
            jax.ShapeDtypeStruct((slots, 2, side // 2, 2, number, channels), jnp.float32),
            jax.ShapeDtypeStruct((count * share, channels), jnp.bfloat16),
        ),
        in_specs=[whole(pltpu.SMEM)] + [whole(pl.ANY)] * 4,
        out_specs=(whole(pl.ANY), whole()),
        scratch_shapes=[
            pltpu.VMEM(images.shape, jnp.bfloat16),
            pltpu.VMEM(images.shape, jnp.bfloat16),
            pltpu.VMEM(kernel.shape, jnp.float32),
            pltpu.VMEM(forward_both.shape, jnp.bfloat16),
            pltpu.VMEM((slots, 2, side // 2, 2 * number, wide), jnp.float32),
            pltpu.VMEM((CHAINS, 2, 4, side // 2, 2 * number, wide), jnp.bfloat16),
            pltpu.VMEM((slots, 4, wide, wide), jnp.bfloat16),
            pltpu.VMEM((4, 3, channels, channels), jnp.float32),
            pltpu.VMEM((3, 3, channels, channels), jnp.float32),
            pltpu.VMEM((slots, 2, side // 2, 2, number, channels), jnp.float32),
            pltpu.VMEM((2 * CHAINS, side * number, wide), jnp.bfloat16),
            pltpu.VMEM((2 * CHAINS, side * number, 3 * wide), jnp.bfloat16),
            pltpu.SemaphoreType.DMA((2, IN_PARTS)),
            pltpu.SemaphoreType.DMA((2,)),
            pltpu.SemaphoreType.DMA((slots,)),
        ],
        compiler_params=params,
        cost_estimate=pl.CostEstimate(
            flops=2 * APPLICATIONS * slots * rows * 3 * wide * wide,
            bytes_accessed=12 * 1024 * 1024,
            transcendentals=0,
        ),
        name="horner_and_gradient",
    )(
        jnp.asarray(slot_factors(side)),
        images,
        cotangent,
        kernel,
        jnp.asarray(forward_both),
    )
    summed = device_sum(partial, 2.0 / (number * count), count)
    outputs = pl.pallas_call(
        inverse_kernel,
        out_shape=jax.ShapeDtypeStruct(images.shape, jnp.bfloat16),
        in_specs=[whole()] * 4,
        out_specs=whole(),
        compiler_params=params,
        cost_estimate=pl.CostEstimate(
            flops=6 * side * side * number * side * number * channels,
            bytes_accessed=8 * 1024 * 1024,
            transcendentals=0,
        ),
        name="inverse_transform",
    )(images, deviation, jnp.asarray(inverse_high), jnp.asarray(inverse_low))
    kernel_grad = pl.pallas_call(
        mirror_kernel,
        out_shape=jax.ShapeDtypeStruct(kernel.shape, jnp.float32),
        in_specs=[whole()],
        out_specs=whole(),
        compiler_params=pltpu.CompilerParams(vmem_limit_bytes=MIRROR_LIMIT),
        name="mirror_taps",
    )(summed)
    return (outputs, kernel_grad)


def solution(mesh):
    split = P(AXES, None, None, None)
    return jax.shard_map(
        per_device,
        mesh=mesh,
        in_specs=(split, split, P()),
        out_specs=(split, P()),
        check_vma=False,
    )
```

```python
import functools
import math

import jax
import jax.numpy as jnp
import numpy as np
from jax import lax
from jax.experimental import pallas as pl
from jax.experimental.pallas import tpu as pltpu
from jax.sharding import PartitionSpec as P

AXES = ("sample", "freq")
APPLICATIONS = 7
CHAINS = 2
IN_PARTS = 4
AHEAD = 2
LAG = 0
GROUPS = 4
HALF_TAPS = ((1, 2), (2, 0), (2, 1), (2, 2))
VMEM_LIMIT = 56 * 1024 * 1024
MIRROR_LIMIT = 4 * 1024 * 1024


def split_table(table):
    high = table.astype(jnp.bfloat16)
    low = (table - high.astype(np.float64)).astype(jnp.bfloat16)
    return high, low


def forward_table(number, side):
    place = np.arange(side)
    table = np.zeros((side, side))
    table[0] = 1.0
    table[1] = np.cos(np.pi * place)
    for slot in range(1, side // 2):
        angle = 2.0 * math.pi * ((slot * place) % side) / side
        table[2 * slot] = np.cos(angle)
        table[2 * slot + 1] = -np.sin(angle)
    full = np.einsum("kw,nm->knmw", table, np.eye(number))
    return full.reshape(side * number, number * side)


def inverse_table(number, side):
    place = np.arange(side)
    table = np.zeros((side, side))
    table[:, 0] = 2.0 / side
    table[:, 1] = 2.0 / side * np.cos(np.pi * place)
    for slot in range(1, side // 2):
        angle = 2.0 * math.pi * ((slot * place) % side) / side
        table[:, 2 * slot] = 4.0 / side * np.cos(angle)
        table[:, 2 * slot + 1] = -4.0 / side * np.sin(angle)
    full = np.einsum("wk,nm->nwkm", table, np.eye(number))
    return full.reshape(number * side, side * number)


def slot_factors(side):
    rows = [[1.0, -1.0, 0.0, 1.0 / side]]
    for slot in range(1, side // 2):
        angle = 2.0 * math.pi * slot / side
        rows.append([math.cos(angle), math.cos(angle), math.sin(angle), 2.0 / side])
    table = np.array(rows)
    weighted = table[:, :3] * table[:, 3:]
    return np.concatenate([table, weighted], axis=1).astype(np.float32)


def dot(left, right):
    return jnp.dot(left, right, preferred_element_type=jnp.float32)


def main_kernel(
    factor_ref,
    x_hbm,
    t_hbm,
    kernel_hbm,
    table_hbm,
    dev_hbm,
    grad_ref,
    x_ref,
    t_ref,
    kernel_ref,
    table_ref,
    base_ref,
    held_ref,
    weight_ref,
    taps_ref,
    sums_ref,
    dev_ref,
    left_ref,
    right_ref,
    in_sems,
    other_sems,
    out_sems,
):
    number, side, _, channels = x_ref.shape
    slots = side // 2
    wide = 2 * channels
    pairs = side // 2
    part = side // IN_PARTS

    def incoming(index, place):
        source, target = ((x_hbm, x_ref), (t_hbm, t_ref))[index]
        rows = pl.ds(place * part, part)
        return pltpu.make_async_copy(
            source.at[:, rows], target.at[:, rows], in_sems.at[index, place]
        )

    def outgoing(slot):
        return pltpu.make_async_copy(dev_ref.at[slot], dev_hbm.at[slot], out_sems.at[slot])

    table_copy = pltpu.make_async_copy(table_hbm, table_ref, other_sems.at[0])
    kernel_copy = pltpu.make_async_copy(kernel_hbm, kernel_ref, other_sems.at[1])
    table_copy.start()
    for place in range(AHEAD):
        for index in range(2):
            incoming(index, place).start()
        if place == 0:
            kernel_copy.start()
    def make_taps():
        for a in range(3):
            flipped = [kernel_ref[a, b].T - kernel_ref[2 - a, 2 - b] for b in range(3)]
            place = 3 - 3 * a // 2 if a != 1 else 1
            taps_ref[place, 0] = -flipped[1]
            taps_ref[place, 1] = -(flipped[2] + flipped[0])
            taps_ref[place, 2] = flipped[2] - flipped[0]
        outside = 0.5 * (taps_ref[0] + taps_ref[3])
        inside = 0.5 * taps_ref[1]
        taps_ref[1] = outside + inside
        taps_ref[2] = outside - inside

    def transform(h):
        rows = jnp.concatenate(
            [
                x_ref[:, h].reshape(number * side, channels),
                t_ref[:, h].reshape(number * side, channels),
            ],
            axis=1,
        )
        result = dot(table_ref[...], rows).reshape(slots, 2, number, wide)
        pair, odd = h // 2, h % 2
        base_ref[:, odd, pair, :number, :channels] = result[:, 0, :, :channels]
        base_ref[:, odd, pair, :number, channels:] = result[:, 1, :, :channels]
        base_ref[:, odd, pair, number:, :channels] = result[:, 0, :, channels:]
        base_ref[:, odd, pair, number:, channels:] = result[:, 1, :, channels:]

    def before_of(rows):
        return jnp.concatenate([rows[pairs - 1 :], rows[: pairs - 1]], axis=0)

    def after_of(rows):
        return jnp.concatenate([rows[1:], rows[:1]], axis=0)

    def store_held(chain, parity, even, odd):
        even, odd = even.astype(jnp.bfloat16), odd.astype(jnp.bfloat16)
        held_ref[chain, parity, 0] = before_of(odd) - odd
        held_ref[chain, parity, 1] = even + odd
        held_ref[chain, parity, 2] = odd - even
        held_ref[chain, parity, 3] = even - after_of(even)

    def prepare_taps(slot, a):
        cos_top, cos_low, sine = (factor_ref[slot, j] for j in range(3))
        first, second = taps_ref[a, 0], taps_ref[a, 1]
        cross = (sine * taps_ref[a, 2]).astype(jnp.bfloat16)
        top = (first + cos_top * second).astype(jnp.bfloat16)
        low = top if slot else (first + cos_low * second).astype(jnp.bfloat16)
        weight_ref[slot, a, :channels, :channels] = top
        weight_ref[slot, a, channels:, channels:] = low
        weight_ref[slot, a, :channels, channels:] = cross
        weight_ref[slot, a, channels:, :channels] = -cross

    def apply(chain, parity, slot):
        def part(place):
            left = held_ref[chain, parity, place].reshape(pairs * 2 * number, wide)
            return dot(left, weight_ref[slot, place]).reshape(pairs, 2 * number, wide)

        first, inner, outer, last = (part(place) for place in range(4))
        return first + (inner + outer), (inner - outer) - last

    def advance(moved, base, step):
        x_new = base[:, :number] + moved[:, :number]
        if step % 2 == 0:
            t_new = moved[:, number:] - base[:, number:]
        else:
            t_new = moved[:, number:] + base[:, number:]
        return x_new, t_new

    def finish(buffer, slot, even, odd, even_new, odd_new):
        for place, moved in enumerate((even, odd)):
            dev_ref[slot, place, :, 0] = moved[:, :number, :channels]
            dev_ref[slot, place, :, 1] = moved[:, :number, channels:]
        half = pairs * number
        even_x, even_t = even_new
        odd_x, odd_t = odd_new
        left_ref[buffer, :half] = even_t.reshape(half, wide).astype(jnp.bfloat16)
        left_ref[buffer, half:] = odd_t.reshape(half, wide).astype(jnp.bfloat16)
        shifted = ((odd_x, after_of(even_x)), (even_x, odd_x), (before_of(odd_x), even_x))
        for a, (top, low) in enumerate(shifted):
            columns = slice(a * wide, (a + 1) * wide)
            right_ref[buffer, :half, columns] = top.reshape(half, wide).astype(jnp.bfloat16)
            right_ref[buffer, half:, columns] = low.reshape(half, wide).astype(jnp.bfloat16)

    def products(buffer, slot):
        weight, top, low, sine = (factor_ref[slot, j] for j in range(3, 7))
        outer_all = lax.dot_general(
            left_ref[buffer],
            right_ref[buffer],
            (((0,), (0,)), ((), ())),
            preferred_element_type=jnp.float32,
        )
        for a in range(3):
            outer = outer_all[:, a * wide : (a + 1) * wide]
            upper, lower = outer[:channels, :channels], outer[channels:, channels:]
            sums_ref[a, 0] += weight * (upper + lower)
            sums_ref[a, 1] += top * upper + low * lower
            sums_ref[a, 2] += sine * (outer[channels:, :channels] - outer[:channels, channels:])

    def work(group, odd):
        here, first = (CHAINS, 1) if odd else (0, 0)
        there = CHAINS - here
        before = jnp.maximum((group - 1) * CHAINS, 0)
        after = jnp.minimum((group + 1) * CHAINS, slots - CHAINS)
        for step in range(APPLICATIONS):
            for chain in range(CHAINS):
                slot = group * CHAINS + chain
                even, odd = apply(chain, (first + step) % 2, slot)
                even_new = advance(even, base_ref[slot, 0], step)
                odd_new = advance(odd, base_ref[slot, 1], step)
                if step < APPLICATIONS - 1:
                    store_held(
                        chain,
                        (first + step + 1) % 2,
                        jnp.concatenate(even_new, axis=1),
                        jnp.concatenate(odd_new, axis=1),
                    )
                else:
                    finish(here + chain, slot, even, odd, even_new, odd_new)
                if step == APPLICATIONS - 2:
                    store_held(
                        chain, 1 - first, base_ref[after + chain, 0], base_ref[after + chain, 1]
                    )
                if step == LAG:
                    products(there + chain, before + chain)

    sums_ref[...] = jnp.zeros_like(sums_ref)
    left_ref[CHAINS:] = jnp.zeros_like(left_ref[CHAINS:])
    right_ref[CHAINS:] = jnp.zeros_like(right_ref[CHAINS:])
    jobs = [(slot, a) for slot in range(slots) for a in range(4)]
    table_copy.wait()
    for place in range(IN_PARTS):
        for index in range(2):
            incoming(index, place).wait()
        if place + AHEAD < IN_PARTS:
            for index in range(2):
                incoming(index, place + AHEAD).start()
        if place == 1:
            kernel_copy.wait()
            make_taps()
        for h in range(place * part, (place + 1) * part):
            transform(h)
            if place:
                turn, turns = h - part, side - part
                for job in jobs[turn * len(jobs) // turns : (turn + 1) * len(jobs) // turns]:
                    prepare_taps(*job)
    for chain in range(CHAINS):
        store_held(chain, 0, base_ref[chain, 0], base_ref[chain, 1])

    def some_groups(index, carry):
        for member in range(GROUPS):
            work(GROUPS * index + member, member % 2 == 1)
            for chain in range(CHAINS):
                outgoing((index * GROUPS + member) * CHAINS + chain).start()
        return carry

    lax.fori_loop(0, slots // (GROUPS * CHAINS), some_groups, 0)
    for chain in range(CHAINS):
        products(CHAINS + chain, slots - CHAINS + chain)

    def correlation(a, b):
        if b == 1:
            return sums_ref[a, 0]
        if b == 2:
            return sums_ref[a, 1] - sums_ref[a, 2]
        return sums_ref[a, 1] + sums_ref[a, 2]

    half = channels // 2
    centre = correlation(1, 1)
    centre = centre - centre.T
    row = lax.broadcasted_iota(jnp.int32, (half, channels), 0)
    lane = lax.broadcasted_iota(jnp.int32, (half, channels), 1)
    packed = jnp.where(lane > row, centre[:half], pltpu.roll(centre[half:], half, 1))
    grad_ref[:half] = packed.astype(grad_ref.dtype)
    for place, (a, b) in enumerate(HALF_TAPS):
        piece = correlation(a, b) - correlation(2 - a, 2 - b).T
        start = half + place * channels
        grad_ref[start : start + channels] = piece.astype(grad_ref.dtype)
    rows = half + len(HALF_TAPS) * channels
    if grad_ref.shape[0] > rows:
        grad_ref[rows:] = jnp.zeros((grad_ref.shape[0] - rows, channels), grad_ref.dtype)
    for slot in range(slots):
        outgoing(slot).wait()


def inverse_kernel(x_ref, dev_ref, high_ref, low_ref, out_ref):
    number, side, _, channels = x_ref.shape

    def transform(pair, carry):
        rows = jnp.concatenate(
            [dev_ref[:, j, pair].reshape(side * number, channels) for j in range(2)], axis=1
        )
        high = rows.astype(jnp.bfloat16)
        low = (rows - high.astype(jnp.float32)).astype(jnp.bfloat16)
        result = dot(high_ref[...], high) + dot(low_ref[...], high) + dot(high_ref[...], low)
        for j in range(2):
            h = 2 * pair + j
            piece = result[:, j * channels : (j + 1) * channels]
            piece = piece.reshape(number, side, channels) + x_ref[:, h].astype(jnp.float32)
            out_ref[:, h] = piece.astype(jnp.bfloat16)
        return carry

    lax.fori_loop(0, side // 2, transform, 0, unroll=2)


def mirror_kernel(sum_ref, grad_ref):
    channels = sum_ref.shape[1]
    half = channels // 2
    packed = sum_ref[:half].astype(jnp.float32)
    row = lax.broadcasted_iota(jnp.int32, (half, channels), 0)
    lane = lax.broadcasted_iota(jnp.int32, (half, channels), 1)
    upper = jnp.where(lane > row, packed, 0.0)
    lower = pltpu.roll(jnp.where(lane < row, packed, 0.0), half, 1)
    once = jnp.concatenate([upper, lower], axis=0)
    grad_ref[1, 1] = once - once.T
    for place, (a, b) in enumerate(HALF_TAPS):
        start = half + place * channels
        piece = sum_ref[start : start + channels].astype(jnp.float32)
        grad_ref[a, b] = piece
        grad_ref[2 - a, 2 - b] = -piece.T


def whole(memory_space=pltpu.VMEM):
    return pl.BlockSpec(memory_space=memory_space)


def device_sum(partial, scale, count):
    pieces = partial.reshape(count, -1, 2, partial.shape[1])
    terms = lax.all_to_all(pieces, AXES, split_axis=0, concat_axis=0, tiled=True)
    own = jnp.sum(scale * terms.astype(jnp.float32), axis=0, keepdims=True).astype(partial.dtype)
    shares = lax.all_to_all(
        jnp.broadcast_to(own, terms.shape), AXES, split_axis=0, concat_axis=0, tiled=True
    )
    return shares.reshape(partial.shape)


def per_device(images, cotangent, kernel):
    number, side, _, channels = images.shape
    slots = side // 2
    wide = 2 * channels
    count = lax.axis_size("sample") * lax.axis_size("freq")
    sent = channels // 2 + len(HALF_TAPS) * channels
    share = -(-sent // (2 * count)) * 2
    forward = forward_table(number, side).astype(jnp.bfloat16)
    inverse_high, inverse_low = split_table(inverse_table(number, side))
    rows = side * 2 * number
    params = pltpu.CompilerParams(vmem_limit_bytes=VMEM_LIMIT)
    deviation, partial = pl.pallas_call(
        main_kernel,
        out_shape=(
            jax.ShapeDtypeStruct((slots, 2, side // 2, 2, number, channels), jnp.float32),
            jax.ShapeDtypeStruct((count * share, channels), jnp.bfloat16),
        ),
        in_specs=[whole(pltpu.SMEM)] + [whole(pl.ANY)] * 4,
        out_specs=(whole(pl.ANY), whole()),
        scratch_shapes=[
            pltpu.VMEM(images.shape, jnp.bfloat16),
            pltpu.VMEM(images.shape, jnp.bfloat16),
            pltpu.VMEM(kernel.shape, jnp.float32),
            pltpu.VMEM(forward.shape, jnp.bfloat16),
            pltpu.VMEM((slots, 2, side // 2, 2 * number, wide), jnp.float32),
            pltpu.VMEM((CHAINS, 2, 4, side // 2, 2 * number, wide), jnp.bfloat16),
            pltpu.VMEM((slots, 4, wide, wide), jnp.bfloat16),
            pltpu.VMEM((4, 3, channels, channels), jnp.float32),
            pltpu.VMEM((3, 3, channels, channels), jnp.float32),
            pltpu.VMEM((slots, 2, side // 2, 2, number, channels), jnp.float32),
            pltpu.VMEM((2 * CHAINS, side * number, wide), jnp.bfloat16),
            pltpu.VMEM((2 * CHAINS, side * number, 3 * wide), jnp.bfloat16),
            pltpu.SemaphoreType.DMA((2, IN_PARTS)),
            pltpu.SemaphoreType.DMA((2,)),
            pltpu.SemaphoreType.DMA((slots,)),
        ],
        compiler_params=params,
        cost_estimate=pl.CostEstimate(
            flops=2 * APPLICATIONS * slots * rows * 3 * wide * wide,
            bytes_accessed=12 * 1024 * 1024,
            transcendentals=0,
        ),
        name="horner_and_gradient",
    )(
        jnp.asarray(slot_factors(side)),
        images,
        cotangent,
        kernel,
        jnp.asarray(forward),
    )
    summed = device_sum(partial, 2.0 / (number * count), count)
    outputs = pl.pallas_call(
        inverse_kernel,
        out_shape=jax.ShapeDtypeStruct(images.shape, jnp.bfloat16),
        in_specs=[whole()] * 4,
        out_specs=whole(),
        compiler_params=params,
        cost_estimate=pl.CostEstimate(
            flops=6 * side * side * number * side * number * channels,
            bytes_accessed=8 * 1024 * 1024,
            transcendentals=0,
        ),
        name="inverse_transform",
    )(images, deviation, jnp.asarray(inverse_high), jnp.asarray(inverse_low))
    kernel_grad = pl.pallas_call(
        mirror_kernel,
        out_shape=jax.ShapeDtypeStruct(kernel.shape, jnp.float32),
        in_specs=[whole()],
        out_specs=whole(),
        compiler_params=pltpu.CompilerParams(vmem_limit_bytes=MIRROR_LIMIT),
        name="mirror_taps",
    )(summed)
    return (outputs, kernel_grad)


def solution(mesh):
    split = P(AXES, None, None, None)
    return jax.shard_map(
        per_device,
        mesh=mesh,
        in_specs=(split, split, P()),
        out_specs=(split, P()),
        check_vma=False,
    )
```

```python
import functools
import math

import jax
import jax.numpy as jnp
import numpy as np
from jax import lax
from jax.experimental import pallas as pl
from jax.experimental.pallas import tpu as pltpu
from jax.sharding import PartitionSpec as P

AXES = ("sample", "freq")
APPLICATIONS = 7
CHAINS = 2
IN_PARTS = 4
AHEAD = 2
LAG = 0
GROUPS = 4
HALF_TAPS = ((1, 2), (2, 0), (2, 1), (2, 2))
VMEM_LIMIT = 56 * 1024 * 1024
MIRROR_LIMIT = 4 * 1024 * 1024


def split_table(table):
    high = table.astype(jnp.bfloat16)
    low = (table - high.astype(np.float64)).astype(jnp.bfloat16)
    return high, low


def forward_table(number, side):
    place = np.arange(side)
    table = np.zeros((side, side))
    table[0] = 1.0
    table[1] = np.cos(np.pi * place)
    for slot in range(1, side // 2):
        angle = 2.0 * math.pi * ((slot * place) % side) / side
        table[2 * slot] = np.cos(angle)
        table[2 * slot + 1] = -np.sin(angle)
    full = np.einsum("kw,nm->knmw", table, np.eye(number))
    return full.reshape(side * number, number * side)


def inverse_table(number, side):
    place = np.arange(side)
    table = np.zeros((side, side))
    table[:, 0] = 2.0 / side
    table[:, 1] = 2.0 / side * np.cos(np.pi * place)
    for slot in range(1, side // 2):
        angle = 2.0 * math.pi * ((slot * place) % side) / side
        table[:, 2 * slot] = 4.0 / side * np.cos(angle)
        table[:, 2 * slot + 1] = -4.0 / side * np.sin(angle)
    full = np.einsum("wk,nm->nwkm", table, np.eye(number))
    return full.reshape(number * side, side * number)


def slot_factors(side):
    rows = [[1.0, -1.0, 0.0, 1.0 / side]]
    for slot in range(1, side // 2):
        angle = 2.0 * math.pi * slot / side
        rows.append([math.cos(angle), math.cos(angle), math.sin(angle), 2.0 / side])
    table = np.array(rows)
    weighted = table[:, :3] * table[:, 3:]
    return np.concatenate([table, weighted], axis=1).astype(np.float32)


def dot(left, right):
    return jnp.dot(left, right, preferred_element_type=jnp.float32)


def main_kernel(
    factor_ref,
    x_hbm,
    t_hbm,
    kernel_hbm,
    table_hbm,
    dev_hbm,
    grad_ref,
    x_ref,
    t_ref,
    kernel_ref,
    table_ref,
    base_ref,
    held_ref,
    weight_ref,
    taps_ref,
    sums_ref,
    dev_ref,
    left_ref,
    right_ref,
    in_sems,
    other_sems,
    out_sems,
):
    number, side, _, channels = x_ref.shape
    slots = side // 2
    wide = 2 * channels
    pairs = side // 2
    part = side // IN_PARTS

    def incoming(index, place):
        source, target = ((x_hbm, x_ref), (t_hbm, t_ref))[index]
        rows = pl.ds(place * part, part)
        return pltpu.make_async_copy(
            source.at[:, rows], target.at[:, rows], in_sems.at[index, place]
        )

    def outgoing(slot):
        return pltpu.make_async_copy(dev_ref.at[slot], dev_hbm.at[slot], out_sems.at[slot])

    table_copy = pltpu.make_async_copy(table_hbm, table_ref, other_sems.at[0])
    kernel_copy = pltpu.make_async_copy(kernel_hbm, kernel_ref, other_sems.at[1])
    table_copy.start()
    for place in range(AHEAD):
        for index in range(2):
            incoming(index, place).start()
        if place == 0:
            kernel_copy.start()
    def make_taps():
        for a in range(3):
            flipped = [kernel_ref[a, b].T - kernel_ref[2 - a, 2 - b] for b in range(3)]
            place = 3 - 3 * a // 2 if a != 1 else 1
            taps_ref[place, 0] = -flipped[1]
            taps_ref[place, 1] = -(flipped[2] + flipped[0])
            taps_ref[place, 2] = flipped[2] - flipped[0]
        outside = 0.5 * (taps_ref[0] + taps_ref[3])
        inside = 0.5 * taps_ref[1]
        taps_ref[1] = outside + inside
        taps_ref[2] = outside - inside

    def transform(h):
        rows = jnp.concatenate(
            [
                x_ref[:, h].reshape(number * side, channels),
                t_ref[:, h].reshape(number * side, channels),
            ],
            axis=1,
        )
        result = dot(table_ref[...], rows).reshape(slots, 2, number, wide)
        pair, odd = h // 2, h % 2
        base_ref[:, odd, pair, :number, :channels] = result[:, 0, :, :channels]
        base_ref[:, odd, pair, :number, channels:] = result[:, 1, :, :channels]
        base_ref[:, odd, pair, number:, :channels] = result[:, 0, :, channels:]
        base_ref[:, odd, pair, number:, channels:] = result[:, 1, :, channels:]

    def before_of(rows):
        return jnp.concatenate([rows[pairs - 1 :], rows[: pairs - 1]], axis=0)

    def after_of(rows):
        return jnp.concatenate([rows[1:], rows[:1]], axis=0)

    def store_held(chain, parity, even, odd):
        even, odd = even.astype(jnp.bfloat16), odd.astype(jnp.bfloat16)
        held_ref[chain, parity, 0] = before_of(odd) - odd
        held_ref[chain, parity, 1] = even + odd
        held_ref[chain, parity, 2] = odd - even
        held_ref[chain, parity, 3] = even - after_of(even)

    def prepare_taps(slot, a):
        cos_top, cos_low, sine = (factor_ref[slot, j] for j in range(3))
        first, second = taps_ref[a, 0], taps_ref[a, 1]
        cross = (sine * taps_ref[a, 2]).astype(jnp.bfloat16)
        top = (first + cos_top * second).astype(jnp.bfloat16)
        low = top if slot else (first + cos_low * second).astype(jnp.bfloat16)
        weight_ref[slot, a, :channels, :channels] = top
        weight_ref[slot, a, channels:, channels:] = low
        weight_ref[slot, a, :channels, channels:] = cross
        weight_ref[slot, a, channels:, :channels] = -cross

    def apply(chain, parity, slot):
        def part(place):
            left = held_ref[chain, parity, place].reshape(pairs * 2 * number, wide)
            return dot(left, weight_ref[slot, place]).reshape(pairs, 2 * number, wide)

        first, inner, outer, last = (part(place) for place in range(4))
        return first + (inner + outer), (inner - outer) - last

    def advance(moved, base, step):
        x_new = base[:, :number] + moved[:, :number]
        if step % 2 == 0:
            t_new = moved[:, number:] - base[:, number:]
        else:
            t_new = moved[:, number:] + base[:, number:]
        return x_new, t_new

    def finish(buffer, slot, even, odd, even_new, odd_new):
        for place, moved in enumerate((even, odd)):
            dev_ref[slot, place, :, 0] = moved[:, :number, :channels]
            dev_ref[slot, place, :, 1] = moved[:, :number, channels:]
        half = pairs * number
        even_x, even_t = even_new
        odd_x, odd_t = odd_new
        left_ref[buffer, :half] = even_t.reshape(half, wide).astype(jnp.bfloat16)
        left_ref[buffer, half:] = odd_t.reshape(half, wide).astype(jnp.bfloat16)
        shifted = ((odd_x, after_of(even_x)), (even_x, odd_x), (before_of(odd_x), even_x))
        for a, (top, low) in enumerate(shifted):
            columns = slice(a * wide, (a + 1) * wide)
            right_ref[buffer, :half, columns] = top.reshape(half, wide).astype(jnp.bfloat16)
            right_ref[buffer, half:, columns] = low.reshape(half, wide).astype(jnp.bfloat16)

    def products(buffer, slot):
        weight, top, low, sine = (factor_ref[slot, j] for j in range(3, 7))
        outer_all = lax.dot_general(
            left_ref[buffer],
            right_ref[buffer],
            (((0,), (0,)), ((), ())),
            preferred_element_type=jnp.float32,
        )
        for a in range(3):
            outer = outer_all[:, a * wide : (a + 1) * wide]
            upper, lower = outer[:channels, :channels], outer[channels:, channels:]
            sums_ref[a, 0] += weight * (upper + lower)
            sums_ref[a, 1] += top * upper + low * lower
            sums_ref[a, 2] += sine * (outer[channels:, :channels] - outer[:channels, channels:])

    def work(group, odd):
        here, first = (CHAINS, 1) if odd else (0, 0)
        there = CHAINS - here
        before = jnp.maximum((group - 1) * CHAINS, 0)
        after = jnp.minimum((group + 1) * CHAINS, slots - CHAINS)
        for step in range(APPLICATIONS):
            for chain in range(CHAINS):
                slot = group * CHAINS + chain
                even, odd = apply(chain, (first + step) % 2, slot)
                even_new = advance(even, base_ref[slot, 0], step)
                odd_new = advance(odd, base_ref[slot, 1], step)
                if step < APPLICATIONS - 1:
                    store_held(
                        chain,
                        (first + step + 1) % 2,
                        jnp.concatenate(even_new, axis=1),
                        jnp.concatenate(odd_new, axis=1),
                    )
                else:
                    finish(here + chain, slot, even, odd, even_new, odd_new)
                if step == APPLICATIONS - 2:
                    store_held(
                        chain, 1 - first, base_ref[after + chain, 0], base_ref[after + chain, 1]
                    )
                if step == LAG:
                    products(there + chain, before + chain)

    jobs = [(slot, a) for slot in range(slots) for a in range(4)]
    table_copy.wait()
    for place in range(IN_PARTS):
        for index in range(2):
            incoming(index, place).wait()
        if place + AHEAD < IN_PARTS:
            for index in range(2):
                incoming(index, place + AHEAD).start()
        if place == 1:
            kernel_copy.wait()
            make_taps()
            sums_ref[...] = jnp.zeros_like(sums_ref)
            left_ref[CHAINS:] = jnp.zeros_like(left_ref[CHAINS:])
            right_ref[CHAINS:] = jnp.zeros_like(right_ref[CHAINS:])
        for h in range(place * part, (place + 1) * part):
            transform(h)
            if place:
                turn, turns = h - part, side - part
                for job in jobs[turn * len(jobs) // turns : (turn + 1) * len(jobs) // turns]:
                    prepare_taps(*job)
    for chain in range(CHAINS):
        store_held(chain, 0, base_ref[chain, 0], base_ref[chain, 1])

    def some_groups(index, carry):
        for member in range(GROUPS):
            work(GROUPS * index + member, member % 2 == 1)
            for chain in range(CHAINS):
                outgoing((index * GROUPS + member) * CHAINS + chain).start()
        return carry

    lax.fori_loop(0, slots // (GROUPS * CHAINS), some_groups, 0)
    for chain in range(CHAINS):
        products(CHAINS + chain, slots - CHAINS + chain)

    def correlation(a, b):
        if b == 1:
            return sums_ref[a, 0]
        if b == 2:
            return sums_ref[a, 1] - sums_ref[a, 2]
        return sums_ref[a, 1] + sums_ref[a, 2]

    half = channels // 2
    centre = correlation(1, 1)
    centre = centre - centre.T
    row = lax.broadcasted_iota(jnp.int32, (half, channels), 0)
    lane = lax.broadcasted_iota(jnp.int32, (half, channels), 1)
    packed = jnp.where(lane > row, centre[:half], pltpu.roll(centre[half:], half, 1))
    grad_ref[:half] = packed.astype(grad_ref.dtype)
    for place, (a, b) in enumerate(HALF_TAPS):
        piece = correlation(a, b) - correlation(2 - a, 2 - b).T
        start = half + place * channels
        grad_ref[start : start + channels] = piece.astype(grad_ref.dtype)
    rows = half + len(HALF_TAPS) * channels
    if grad_ref.shape[0] > rows:
        grad_ref[rows:] = jnp.zeros((grad_ref.shape[0] - rows, channels), grad_ref.dtype)
    for slot in range(slots):
        outgoing(slot).wait()


def inverse_kernel(x_ref, dev_ref, high_ref, low_ref, out_ref):
    number, side, _, channels = x_ref.shape

    def transform(pair, carry):
        rows = jnp.concatenate(
            [dev_ref[:, j, pair].reshape(side * number, channels) for j in range(2)], axis=1
        )
        high = rows.astype(jnp.bfloat16)
        low = (rows - high.astype(jnp.float32)).astype(jnp.bfloat16)
        result = dot(high_ref[...], high) + dot(low_ref[...], high) + dot(high_ref[...], low)
        for j in range(2):
            h = 2 * pair + j
            piece = result[:, j * channels : (j + 1) * channels]
            piece = piece.reshape(number, side, channels) + x_ref[:, h].astype(jnp.float32)
            out_ref[:, h] = piece.astype(jnp.bfloat16)
        return carry

    lax.fori_loop(0, side // 2, transform, 0, unroll=2)


def mirror_kernel(sum_ref, grad_ref):
    channels = sum_ref.shape[1]
    half = channels // 2
    packed = sum_ref[:half].astype(jnp.float32)
    row = lax.broadcasted_iota(jnp.int32, (half, channels), 0)
    lane = lax.broadcasted_iota(jnp.int32, (half, channels), 1)
    upper = jnp.where(lane > row, packed, 0.0)
    lower = pltpu.roll(jnp.where(lane < row, packed, 0.0), half, 1)
    once = jnp.concatenate([upper, lower], axis=0)
    grad_ref[1, 1] = once - once.T
    for place, (a, b) in enumerate(HALF_TAPS):
        start = half + place * channels
        piece = sum_ref[start : start + channels].astype(jnp.float32)
        grad_ref[a, b] = piece
        grad_ref[2 - a, 2 - b] = -piece.T


def whole(memory_space=pltpu.VMEM):
    return pl.BlockSpec(memory_space=memory_space)


def device_sum(partial, scale, count):
    pieces = partial.reshape(count, -1, 2, partial.shape[1])
    terms = lax.all_to_all(pieces, AXES, split_axis=0, concat_axis=0, tiled=True)
    own = jnp.sum(scale * terms.astype(jnp.float32), axis=0, keepdims=True).astype(partial.dtype)
    shares = lax.all_to_all(
        jnp.broadcast_to(own, terms.shape), AXES, split_axis=0, concat_axis=0, tiled=True
    )
    return shares.reshape(partial.shape)


def per_device(images, cotangent, kernel):
    number, side, _, channels = images.shape
    slots = side // 2
    wide = 2 * channels
    count = lax.axis_size("sample") * lax.axis_size("freq")
    sent = channels // 2 + len(HALF_TAPS) * channels
    share = -(-sent // (2 * count)) * 2
    forward = forward_table(number, side).astype(jnp.bfloat16)
    inverse_high, inverse_low = split_table(inverse_table(number, side))
    rows = side * 2 * number
    params = pltpu.CompilerParams(vmem_limit_bytes=VMEM_LIMIT)
    deviation, partial = pl.pallas_call(
        main_kernel,
        out_shape=(
            jax.ShapeDtypeStruct((slots, 2, side // 2, 2, number, channels), jnp.float32),
            jax.ShapeDtypeStruct((count * share, channels), jnp.bfloat16),
        ),
        in_specs=[whole(pltpu.SMEM)] + [whole(pl.ANY)] * 4,
        out_specs=(whole(pl.ANY), whole()),
        scratch_shapes=[
            pltpu.VMEM(images.shape, jnp.bfloat16),
            pltpu.VMEM(images.shape, jnp.bfloat16),
            pltpu.VMEM(kernel.shape, jnp.float32),
            pltpu.VMEM(forward.shape, jnp.bfloat16),
            pltpu.VMEM((slots, 2, side // 2, 2 * number, wide), jnp.float32),
            pltpu.VMEM((CHAINS, 2, 4, side // 2, 2 * number, wide), jnp.bfloat16),
            pltpu.VMEM((slots, 4, wide, wide), jnp.bfloat16),
            pltpu.VMEM((4, 3, channels, channels), jnp.float32),
            pltpu.VMEM((3, 3, channels, channels), jnp.float32),
            pltpu.VMEM((slots, 2, side // 2, 2, number, channels), jnp.float32),
            pltpu.VMEM((2 * CHAINS, side * number, wide), jnp.bfloat16),
            pltpu.VMEM((2 * CHAINS, side * number, 3 * wide), jnp.bfloat16),
            pltpu.SemaphoreType.DMA((2, IN_PARTS)),
            pltpu.SemaphoreType.DMA((2,)),
            pltpu.SemaphoreType.DMA((slots,)),
        ],
        compiler_params=params,
        cost_estimate=pl.CostEstimate(
            flops=2 * APPLICATIONS * slots * rows * 3 * wide * wide,
            bytes_accessed=12 * 1024 * 1024,
            transcendentals=0,
        ),
        name="horner_and_gradient",
    )(
        jnp.asarray(slot_factors(side)),
        images,
        cotangent,
        kernel,
        jnp.asarray(forward),
    )
    summed = device_sum(partial, 2.0 / (number * count), count)
    outputs = pl.pallas_call(
        inverse_kernel,
        out_shape=jax.ShapeDtypeStruct(images.shape, jnp.bfloat16),
        in_specs=[whole()] * 4,
        out_specs=whole(),
        compiler_params=params,
        cost_estimate=pl.CostEstimate(
            flops=6 * side * side * number * side * number * channels,
            bytes_accessed=8 * 1024 * 1024,
            transcendentals=0,
        ),
        name="inverse_transform",
    )(images, deviation, jnp.asarray(inverse_high), jnp.asarray(inverse_low))
    kernel_grad = pl.pallas_call(
        mirror_kernel,
        out_shape=jax.ShapeDtypeStruct(kernel.shape, jnp.float32),
        in_specs=[whole()],
        out_specs=whole(),
        compiler_params=pltpu.CompilerParams(vmem_limit_bytes=MIRROR_LIMIT),
        name="mirror_taps",
    )(summed)
    return (outputs, kernel_grad)


def solution(mesh):
    split = P(AXES, None, None, None)
    return jax.shard_map(
        per_device,
        mesh=mesh,
        in_specs=(split, split, P()),
        out_specs=(split, P()),
        check_vma=False,
    )
```
